128 devices in a mesh: section: 4 (over x_lo, core), expert: 32 (over z, y, x_hi).
Axes of the slice: x: 4 (x_hi: 2, x_lo: 2; x = x_hi * 2 + x_lo), y: 4, z: 4, core: 2. Of those that a mesh axis runs over, the one named last changes fastest.
Arguments:
- fwd_in: bfloat16 [4, 2048, 7168], P('section', 'expert'), may hold values from -6 to 6
- gains: float32 [4, 7168], P('section'), may hold values from 0.25 to 1.75
- gate_weight: bfloat16 [4, 7168, 8192], P('section', None, 'expert'), may hold values from -0.0625 to 0.0625
- up_weight: bfloat16 [4, 7168, 8192], P('section', None, 'expert'), may hold values from -0.0625 to 0.0625
- down_weight: bfloat16 [4, 8192, 7168], P('section', 'expert'), may hold values from -0.1875 to 0.1875
- fwd_routes: int32 [4, 2048, 2], P('section', 'expert'), may hold values from 0 to 7, all different within a row; in each aligned block of 64 rows (0 to 63, 64 to 127, ..., all dimensions but the last counted through in order) at most 20 rows name the same one
- fwd_probs: float32 [4, 2048, 2], P('section', 'expert'), may hold values from 0.1 to 1
- bwd_grad: bfloat16 [4, 2048, 7168], P('section', 'expert'), may hold values from -6 to 6
- bwd_input: bfloat16 [4, 2048, 7168], P('section', 'expert'), may hold values from -6 to 6
- bwd_routes: int32 [4, 2048, 2], P('section', 'expert'), may hold values from 0 to 7, all different within a row; in each aligned block of 64 rows (0 to 63, 64 to 127, ..., all dimensions but the last counted through in order) at most 20 rows name the same one
- bwd_probs: float32 [4, 2048, 2], P('section', 'expert'), may hold values from 0.1 to 1
- bwd_stash: bfloat16 [4, 20480, 512], P('section', 'expert'), may hold values from -6 to 6
Outputs:
- fwd_out: bfloat16 [4, 2048, 7168], P('section', 'expert')
- bwd_out: bfloat16 [4, 2048, 7168], P('section', 'expert')
The draws below stay inside these ranges and needn't reach their ends.
Inputs may be any that keep to these rules, and one draw needn't show every extreme that they name: `fwd_routes`: each row names 2 different experts; in the rows of one device no expert is named by more than 20 rows, and in every draw some expert is named by exactly 20 rows of some device. `bwd_routes`: each row names 2 different experts; in the rows of one device no expert is named by more than 20 rows, and in every draw some expert is named by exactly 20 rows of some device.
All inputs are finite; a program needn't handle non-finite values.
Results may differ from the reference program's by a relative error of at most 0.0048.
Values may be sent and summed in bfloat16 or wider, within the bound.
A program may use at most 192 MiB of HBM per device.

```python
import math
import jax
import jax.numpy as jnp
import numpy as np
from jax import lax

D = 7168
HIDDEN_SIZE = 1024
SPLIT = 4
TOPK = 2
TOK_DEV = 64
HID_DEV = 256
EXPERTS = 8
CAP = 20
SECTIONS = 4
TOKENS = 2048
N_EXPERT = 32


def block_levels(stream_key, shape, split, low, largest):
    def one(axis_at, parts):
        draws = jax.random.uniform(jax.random.fold_in(jax.random.fold_in(stream_key, 6), axis_at), (parts,), jnp.float32, low / len(split), largest / len(split))
        return jnp.repeat(jnp.exp(draws), shape[axis_at] // parts).reshape((-1,) + (1,) * (len(shape) - axis_at - 1))

    gain = one(*split[0])
    for cut in split[1:]:
        gain = gain * one(*cut)
    return gain


def deal_out(stream_key, own, number, rows, amount, top, reach, slope):
    ranking = jax.random.permutation(stream_key, amount)
    heavy_load, common = load_shares(amount, rows * top, reach, slope, True), load_shares(amount, rows * top, reach, slope, False)
    places = jnp.arange(amount)

    def named(lengths, rotation):
        used = int((lengths > 0).sum())
        fixed = max(1, used // 4)
        moved = fixed + (places - fixed + rotation * (used - fixed)) % max(1, amount - fixed)
        return jnp.zeros((amount,), jnp.int32).at[ranking[jnp.where(places < fixed, places, moved)]].set(jnp.asarray(lengths, jnp.int32))

    lengths = jnp.where(number % 4 == 0, named(heavy_load, number // 4), named(common, number - number // 4 - 1))
    mixed = jax.random.permutation(jax.random.fold_in(own, 3), amount)
    source_of, taker = mixed[0:amount // 2 * 2:2], mixed[1:amount // 2 * 2:2]
    slack = jnp.minimum(lengths[source_of] - 1, reach - lengths[taker]) // 2
    slack = jnp.where((source_of == ranking[0]) | (taker == ranking[0]) | (lengths[taker] == 0), 0, jnp.maximum(slack, 0))
    moved = jax.random.randint(jax.random.fold_in(own, 4), (amount // 2,), 0, 1 << 20) % (slack + 1)
    lengths = lengths.at[source_of].add(-moved).at[taker].add(moved)
    members = jnp.searchsorted(jnp.cumsum(lengths), jnp.arange(rows * top), side="right").astype(jnp.int32)
    grid = members.reshape(top, rows).T
    grid = grid[jax.random.permutation(jax.random.fold_in(own, 1), rows)]
    rotation = jax.random.randint(jax.random.fold_in(own, 2), (rows, 1), 0, top)
    return jnp.take_along_axis(grid, (jnp.arange(top)[None, :] + rotation) % top, axis=1)


def load_shares(number_of, total, limit, slope, full):
    loads = [(1 << 20) // math.isqrt(grade ** slope) + 1 for grade in range(1, number_of + 1)]
    largest = limit if full else min(limit, max(-(-total // number_of), total * loads[0] // sum(loads)))
    least = 1 if total - largest >= number_of - 1 else 0
    given, surplus = [largest] + [least] * (number_of - 1), total - largest - least * (number_of - 1)
    while surplus > 0:
        movable = [i for i in range(1, number_of) if given[i] < largest] or [i for i in range(1, number_of) if given[i] < limit]
        pool, budget = sum([loads[i] for i in movable]), surplus
        for i in movable:
            more = min(limit - given[i], max(1, budget * loads[i] // pool), surplus)
            given[i] = given[i] + more
            surplus = surplus - more
    return np.array(given)


def scatter_about(rng, dims, spread, bound, shards=(), kind=jnp.bfloat16):
    factor_of = block_levels(rng, dims, shards, -0.22, 0.18) if shards else 1.0
    drawn = jax.random.normal(rng, dims, jnp.float32) * spread * factor_of
    return jnp.minimum(jnp.maximum(drawn, -bound), bound).astype(kind)


def setup_inputs(seed: int = 0) -> dict:
    arg_keys = jax.random.split(jax.random.key(seed), 13)
    fwd_in = scatter_about(arg_keys[0], (SECTIONS, TOKENS, D), 1.0, 6.0, ((0, 4), (1, 32)))
    gains = jnp.clip(1.0 + 0.15 * jax.random.normal(arg_keys[1], (SECTIONS, D), jnp.float32), 0.25, 1.75)
    gate_weight = scatter_about(arg_keys[2], (SECTIONS, D, EXPERTS * HIDDEN_SIZE), D ** -0.5, 0.0625, ((0, 4), (2, 32)))
    up_weight = scatter_about(arg_keys[3], (SECTIONS, D, EXPERTS * HIDDEN_SIZE), D ** -0.5, 0.0625, ((0, 4), (2, 32)))
    down_weight = scatter_about(arg_keys[4], (SECTIONS, EXPERTS * HIDDEN_SIZE, D), HIDDEN_SIZE ** -0.5, 0.1875, ((0, 4), (1, 32)))
    fwd_routes_keys = jax.random.split(jax.random.fold_in(arg_keys[5], 1), SECTIONS * TOKENS // TOK_DEV)
    fwd_routes_turns = jax.random.permutation(jax.random.fold_in(arg_keys[5], 3), SECTIONS * TOKENS // TOK_DEV)
    fwd_routes = jax.vmap(lambda own, number: deal_out(jax.random.fold_in(arg_keys[5], 2), own, number, TOK_DEV, EXPERTS, TOPK, CAP, 2))(fwd_routes_keys, fwd_routes_turns).reshape((SECTIONS, TOKENS, TOPK))
    fwd_probs = jnp.clip(jnp.exp(math.log(1.0) - 2.3025851 * jax.random.uniform(arg_keys[6], (SECTIONS, TOKENS, TOPK), jnp.float32) ** block_levels(arg_keys[6], (SECTIONS, TOKENS, TOPK), ((0, 4), (1, 32)), -0.2, 0.2)), 0.1, 1.0)
    bwd_grad = scatter_about(arg_keys[7], (SECTIONS, TOKENS, D), 1.0, 6.0, ((0, 4), (1, 32)))
    bwd_input = scatter_about(arg_keys[8], (SECTIONS, TOKENS, D), 1.0, 6.0, ((0, 4), (1, 32)))
    bwd_routes_keys = jax.random.split(jax.random.fold_in(arg_keys[9], 1), SECTIONS * TOKENS // TOK_DEV)
    bwd_routes_turns = jax.random.permutation(jax.random.fold_in(arg_keys[9], 3), SECTIONS * TOKENS // TOK_DEV)
    bwd_routes = jax.vmap(lambda own, number: deal_out(jax.random.fold_in(arg_keys[9], 2), own, number, TOK_DEV, EXPERTS, TOPK, CAP, 2))(bwd_routes_keys, bwd_routes_turns).reshape((SECTIONS, TOKENS, TOPK))
    bwd_probs = jnp.clip(jnp.exp(math.log(1.0) - 2.3025851 * jax.random.uniform(arg_keys[10], (SECTIONS, TOKENS, TOPK), jnp.float32) ** block_levels(arg_keys[10], (SECTIONS, TOKENS, TOPK), ((0, 4), (1, 32)), -0.2, 0.2)), 0.1, 1.0)
    bwd_stash = scatter_about(arg_keys[11], (SECTIONS, N_EXPERT * N_EXPERT * CAP, 2 * HID_DEV), 1.0, 6.0, ((0, 4), (1, 32)))
    return dict(fwd_in=fwd_in, gains=gains, gate_weight=gate_weight, up_weight=up_weight, down_weight=down_weight, fwd_routes=fwd_routes, fwd_probs=fwd_probs, bwd_grad=bwd_grad, bwd_input=bwd_input, bwd_routes=bwd_routes, bwd_probs=bwd_probs, bwd_stash=bwd_stash)


EPSILON = 1e-06

def rms_scale(hidden_state, norm_gain):
    return hidden_state * lax.rsqrt(lax.optimization_barrier(jnp.mean(hidden_state * hidden_state, axis=-1, keepdims=True)) + EPSILON) * norm_gain

def place_rows(routes, row_block):
    expert_ids = routes.reshape(N_EXPERT, TOK_DEV * TOPK).astype(jnp.int32)
    onehot = (expert_ids[:, :, None] == jnp.arange(EXPERTS, dtype=jnp.int32)[None, None, :]).astype(jnp.int32)
    before = jnp.cumsum(onehot, axis=1) - onehot
    position = lax.optimization_barrier(jnp.sum(before * onehot, axis=2)).astype(jnp.int32)
    source_ids = jnp.broadcast_to(jnp.arange(N_EXPERT, dtype=jnp.int32)[:, None], expert_ids.shape)
    token_ids = jnp.broadcast_to((jnp.arange(TOK_DEV * TOPK, dtype=jnp.int32) // TOPK)[None, :], expert_ids.shape)
    picked = row_block.reshape(N_EXPERT, TOK_DEV, D)[source_ids, token_ids]
    buffer = jnp.zeros((N_EXPERT, EXPERTS, CAP, D), jnp.bfloat16).at[source_ids, expert_ids, position].set(picked)
    return (buffer, source_ids, expert_ids, position)

def gather_back(results, source_ids, expert_ids, position, probs):
    picked = results[source_ids, expert_ids, position].reshape(TOKENS, TOPK, D)
    return lax.optimization_barrier(jnp.sum(picked * probs[:, :, None].astype(jnp.float32), axis=1))

def reference(fwd_in, gains, gate_weight, up_weight, down_weight, fwd_routes, fwd_probs, bwd_grad, bwd_input, bwd_routes, bwd_probs, bwd_stash):
    forward_list = []
    backward_list = []
    for section_id in range(SECTIONS):
        hidden_state = fwd_in[(section_id - 1) % SECTIONS]
        normed = rms_scale(hidden_state.astype(jnp.float32), gains[section_id]).astype(jnp.bfloat16)
        buffer, source_ids, expert_ids, position = place_rows(fwd_routes[section_id], normed)
        expert_outs = []
        for expert_id in range(EXPERTS):
            row_block = buffer[:, expert_id].reshape(N_EXPERT * CAP, D)
            total = jnp.zeros((N_EXPERT * CAP, D), jnp.float32)
            for part_id in range(SPLIT):
                start = (expert_id * SPLIT + part_id) * HID_DEV
                gate = jnp.dot(row_block, gate_weight[section_id][:, start:start + HID_DEV], preferred_element_type=jnp.float32)
                upper = jnp.dot(row_block, up_weight[section_id][:, start:start + HID_DEV], preferred_element_type=jnp.float32)
                hidden = (jax.nn.silu(gate) * upper).astype(jnp.bfloat16)
                partial_out = jnp.dot(hidden, down_weight[section_id][start:start + HID_DEV], preferred_element_type=jnp.float32).astype(jnp.bfloat16)
                total = total + partial_out.astype(jnp.float32)
            expert_outs.append(total.reshape(N_EXPERT, CAP, D))
        results = jnp.stack(expert_outs, axis=1)
        mixture = gather_back(results, source_ids, expert_ids, position, fwd_probs[section_id])
        forward_list.append((hidden_state.astype(jnp.float32) + mixture).astype(jnp.bfloat16))
        upstream = bwd_grad[(section_id + 1) % SECTIONS]
        buffer, source_ids, expert_ids, position = place_rows(bwd_routes[section_id], upstream)
        stash = bwd_stash[section_id].reshape(N_EXPERT, N_EXPERT * CAP, 2 * HID_DEV)
        expert_grads = []
        for expert_id in range(EXPERTS):
            row_block = buffer[:, expert_id].reshape(N_EXPERT * CAP, D)
            total = jnp.zeros((N_EXPERT * CAP, D), jnp.float32)
            for part_id in range(SPLIT):
                device_id = expert_id * SPLIT + part_id
                start = device_id * HID_DEV
                gate_pre = stash[device_id, :, :HID_DEV].astype(jnp.float32)
                up_pre = stash[device_id, :, HID_DEV:].astype(jnp.float32)
                grad_hidden = jnp.dot(row_block, down_weight[section_id][start:start + HID_DEV].T, preferred_element_type=jnp.float32)
                sigmoid_a = jax.nn.sigmoid(gate_pre)
                grad_gate = (grad_hidden * up_pre * sigmoid_a * (1.0 + gate_pre * (1.0 - sigmoid_a))).astype(jnp.bfloat16)
                grad_up = (grad_hidden * gate_pre * sigmoid_a).astype(jnp.bfloat16)
                part_grad = jnp.dot(grad_gate, gate_weight[section_id][:, start:start + HID_DEV].T, preferred_element_type=jnp.float32)
                part_grad = part_grad + jnp.dot(grad_up, up_weight[section_id][:, start:start + HID_DEV].T, preferred_element_type=jnp.float32)
                total = total + part_grad.astype(jnp.bfloat16).astype(jnp.float32)
            expert_grads.append(total.reshape(N_EXPERT, CAP, D))
        results = jnp.stack(expert_grads, axis=1)
        grad_normed = gather_back(results, source_ids, expert_ids, position, bwd_probs[section_id])
        norm_gain = gains[section_id]
        _, pullback = jax.vjp(lambda value: rms_scale(value, norm_gain), bwd_input[section_id].astype(jnp.float32))
        grad_input = pullback(grad_normed)[0]
        backward_list.append((upstream.astype(jnp.float32) + grad_input).astype(jnp.bfloat16))
    return (jnp.stack(forward_list, axis=0), jnp.stack(backward_list, axis=0))
```

```python
import functools

import jax
import jax.numpy as jnp
import numpy as np
from jax import lax
from jax.experimental import pallas as pl
from jax.experimental.pallas import tpu as pltpu
from jax.sharding import PartitionSpec as P

EPSILON = 1e-06
MESH = pl.DeviceIdType.MESH
CAP = 20
CHUNK = 1024
PIECE = 512
NT = (((1,), (1,)), ((), ()))


def mm(a, b):
    return jnp.dot(a, b, preferred_element_type=jnp.float32)


def mm_t(a, b):
    return lax.dot_general(a, b, NT, preferred_element_type=jnp.float32)


def slot_keys(routes, offset):
    tokens = routes.shape[0]
    lane = lax.broadcasted_iota(jnp.int32, (tokens, 128), 1)
    first, second = routes[:, 0:1], routes[:, 1:2]
    one0 = jnp.where(first == lane, 1.0, 0.0)
    one1 = jnp.where(second == lane, 1.0, 0.0)
    row = lax.broadcasted_iota(jnp.int32, (tokens, tokens), 0)
    col = lax.broadcasted_iota(jnp.int32, (tokens, tokens), 1)
    lower = jnp.where(col < row, 1.0, 0.0).astype(jnp.bfloat16)
    before = mm(lower, (one0 + one1).astype(jnp.bfloat16))
    pos0 = jnp.sum(one0 * before, axis=1, keepdims=True)
    pos1 = jnp.sum(one1 * before, axis=1, keepdims=True)
    key0 = first.astype(jnp.float32) * CAP + pos0 + offset
    key1 = second.astype(jnp.float32) * CAP + pos1 + offset
    return key0, key1


def kernel(
    fwd_in, bwd_grad, gains, wg, wu, wd, f_routes, f_probs, b_routes, b_probs, bwd_input, stash, target,
    fwd_out, bwd_out,
    meta, dense, packed, rows, back, o_recv, x_recv, wd_own, wd_peer, w_own, w_peer,
    st_own, st_peer, acc, small, hid, pack, comb, pend, pend2, grad,
    relay_s, relay_r, meta_s, meta_r, o_s, o_r, z_s, z_r, wt_s, wt_r, wd_s, wd_r, st_s, st_r,
    zb_s, zb_r, ob_s, ob_r, xb_s, xb_r, loc, zloc, wloc, zbloc,
):
    depth = fwd_in.shape[1]
    chunks = depth // CHUNK
    hidden = wg.shape[1]
    sec = lax.axis_index("section")
    ex = lax.axis_index("expert")
    z, y, x = ex // 8, (ex // 2) % 4, ex % 2
    half = y // 2
    cls = ((y + 1) // 2) % 2
    own = pl.multiple_of(half * 128, 128)
    other = pl.multiple_of((1 - half) * 128, 128)
    mine = pl.multiple_of(half * 128 + x * 64, 64)
    up, down = (sec + 1) % 4, (sec + 3) % 4

    def at(zz, yy, xx):
        return zz * 8 + yy * 2 + xx

    x_peer = (sec, at(z, y, 1 - x))
    o_peer = (sec, at(z, 3 - y, x))
    d_peer = (sec, at(z, 3 - y, 1 - x))
    i_peer = (sec, at(z, y + 1 - 2 * (y % 2), x))
    z_peers = [(sec, at((z + d) % 4, y, x)) for d in (1, 2, 3)]
    relays = [(s, at(z, y, xx)) for s in (up, down) for xx in (x, 1 - x)]

    barrier = pltpu.get_barrier_semaphore()
    partners = [x_peer, o_peer, d_peer, i_peer] + z_peers + relays
    for peer in partners:
        pl.semaphore_signal(barrier, inc=1, device_id=peer, device_id_type=MESH)
    pl.semaphore_wait(barrier, len(partners))

    def remote(src, dst, send, recv, peer):
        return pltpu.make_async_remote_copy(
            src_ref=src, dst_ref=dst, send_sem=send, recv_sem=recv, device_id=peer, device_id_type=MESH
        )

    def relay(flow):
        src = (bwd_grad, fwd_in)[flow]
        sec_to = (down, up)[flow]
        return [
            remote(src, dense.at[flow, pl.ds(mine, 64)], relay_s.at[flow, d], relay_r.at[flow, d], (sec_to, at(z, y, xx)))
            for d, xx in enumerate((x, 1 - x))
        ]

    bwd_relay, fwd_relay = relay(0), relay(1)
    for copy in bwd_relay:
        copy.start()
    st_copy = remote(
        stash.at[pl.ds(pl.multiple_of((1 - cls) * 320, 320), 320)], st_peer, st_s, st_r, i_peer
    )
    st_copy.start()
    wd_copy = remote(wd, wd_peer, wd_s, wd_r, i_peer)
    wd_copy.start()

    def w_copies(c):
        at_c = pl.ds(pl.multiple_of(c * CHUNK, CHUNK), CHUNK)
        return [
            remote(w.at[at_c], w_peer.at[k, at_c], wt_s.at[k, c], wt_r.at[k, c], i_peer)
            for k, w in enumerate((wg, wu))
        ]

    def w_send(c):
        for copy in w_copies(c):
            copy.start()

    def w_load(c):
        at_c = pl.ds(pl.multiple_of(c * CHUNK, CHUNK), CHUNK)
        return [
            pltpu.make_async_copy(w.at[at_c], w_own.at[c % 2, k], wloc.at[c % 2, k])
            for k, w in enumerate((wg, wu))
        ]

    st_load = pltpu.make_async_copy(stash.at[pl.ds(pl.multiple_of(cls * 320, 320), 320)], st_own, loc.at[0])
    st_load.start()
    wd_load = pltpu.make_async_copy(wd, wd_own, loc.at[1])
    wd_load.start()
    for copy in w_load(0):
        copy.start()

    lane = lax.broadcasted_iota(jnp.int32, (64, 128), 1)
    offset = ((half * 2 + x) * 1000).astype(jnp.float32)
    columns = []
    for routes, probs in ((b_routes, b_probs), (f_routes, f_probs)):
        key0, key1 = slot_keys(routes[...], offset)
        columns += [key0, key1, probs[:, 0:1], probs[:, 1:2]]
    value = jnp.zeros((64, 128), jnp.float32)
    for i, column in enumerate(columns):
        value = jnp.where(lane == i, column, value)
    meta[pl.ds(mine, 64)] = value
    meta_copies = [
        remote(meta.at[pl.ds(mine, 64)], meta.at[pl.ds(mine, 64)], meta_s.at[i], meta_r.at[i], peer)
        for i, peer in enumerate((x_peer, o_peer, d_peer))
    ]
    for copy in meta_copies:
        copy.start()

    def o_copy(flow):
        block = dense.at[flow, pl.ds(own, 128)]
        return remote(block, block, o_s.at[flow], o_r.at[flow], o_peer)

    for copy in bwd_relay:
        copy.wait()
    o_copy(0).start()
    for copy in fwd_relay:
        copy.start()
    w_send(0)
    bwd_out[...] = dense[0, pl.ds(mine, 64)]

    for copy in meta_copies:
        copy.wait()
    goal = target[...] + (half * CAP).astype(jnp.float32)
    for flow in range(2):
        base = flow * 4
        one0 = jnp.where(meta[:, base : base + 1] == goal, 1.0, 0.0)
        one1 = jnp.where(meta[:, base + 1 : base + 2] == goal, 1.0, 0.0)
        pack[flow] = jnp.transpose(one0 + one1).astype(jnp.bfloat16)
        weight = one0 * meta[:, base + 2 : base + 3] + one1 * meta[:, base + 3 : base + 4]
        high = weight.astype(jnp.bfloat16)
        comb[flow, 0] = high
        comb[flow, 1] = (weight - high.astype(jnp.float32)).astype(jnp.bfloat16)

    for copy in fwd_relay:
        copy.wait()
    fwd_out[...] = dense[1, pl.ds(mine, 64)]

    def norm_rows(i, carry):
        at_i = pl.ds(pl.multiple_of(half * 128 + i * 16, 16), 16)
        v = dense[1, at_i].astype(jnp.float32)
        scale = lax.rsqrt(jnp.mean(v * v, axis=1, keepdims=True) + EPSILON)
        dense[1, at_i] = (v * scale * gains[...]).astype(jnp.bfloat16)
        return carry

    lax.fori_loop(0, 8, norm_rows, 0)
    o_copy(1).start()
    w_send(1)

    def z_copies(flow):
        return [
            remote(
                packed.at[pl.ds(pl.multiple_of(((z + d) % 4) * 80, 80), 80)],
                rows.at[flow, pl.ds(pl.multiple_of(z * 80, 80), 80)],
                z_s.at[flow, d - 1], z_r.at[flow, d - 1], z_peers[d - 1],
            )
            for d in (1, 2, 3)
        ]

    def z_local(flow):
        at_z = pl.ds(pl.multiple_of(z * 80, 80), 80)
        return pltpu.make_async_copy(packed.at[at_z], rows.at[flow, at_z], zloc.at[flow])

    def pack_rows(flow):
        def step(c, carry):
            at_c = pl.ds(pl.multiple_of(c * PIECE, PIECE), PIECE)
            packed[:, at_c] = mm(pack[flow, 0:320], dense[flow, :, at_c]).astype(jnp.bfloat16)
            return carry

        lax.fori_loop(0, depth // PIECE, step, 0)
        for copy in z_copies(flow):
            copy.start()
        z_local(flow).start()

    o_copy(0).wait()
    pack_rows(0)
    w_send(2)
    o_copy(1).wait()
    for copy in z_copies(0):
        copy.wait_send()
    z_local(0).wait()
    pack_rows(1)
    w_send(3)

    for copy in z_copies(0):
        copy.wait_recv()
    wd_load.wait()
    wd_copy.wait()
    acc[...] = jnp.zeros_like(acc)

    def hid_grad(c, carry):
        at_c = pl.ds(pl.multiple_of(c * CHUNK, CHUNK), CHUNK)
        block = rows[0, :, at_c]
        acc[0, 0] += mm_t(block, wd_own[:, at_c])
        acc[0, 1] += mm_t(block, wd_peer[:, at_c])
        return carry

    lax.fori_loop(0, chunks, hid_grad, 0)
    st_load.wait()
    st_copy.wait()
    for k, st in enumerate((st_own, st_peer)):
        a = st[:, 0:hidden].astype(jnp.float32)
        b = st[:, hidden : 2 * hidden].astype(jnp.float32)
        sig = jax.nn.sigmoid(a)
        g = acc[0, k]
        small[0, k] = (g * b * sig * (1.0 + a * (1.0 - sig))).astype(jnp.bfloat16)
        small[1, k] = (g * a * sig).astype(jnp.bfloat16)
    acc[...] = jnp.zeros_like(acc)

    u_load = pltpu.make_async_copy(bwd_input, packed.at[0:64], loc.at[2])

    def zb_copies(q):
        flow, c = q // chunks, q % chunks
        at_c = pl.ds(pl.multiple_of(c * CHUNK, CHUNK), CHUNK)
        return [
            remote(
                rows.at[flow, pl.ds(pl.multiple_of(((z + d) % 4) * 80, 80), 80), at_c],
                back.at[flow, pl.ds(pl.multiple_of(z * 80, 80), 80), at_c],
                zb_s.at[q, d - 1], zb_r.at[q, d - 1], z_peers[d - 1],
            )
            for d in (1, 2, 3)
        ]

    def zb_local(q):
        flow, c = q // chunks, q % chunks
        at_c = pl.ds(pl.multiple_of(c * CHUNK, CHUNK), CHUNK)
        at_z = pl.ds(pl.multiple_of(z * 80, 80), 80)
        return pltpu.make_async_copy(rows.at[flow, at_z, at_c], back.at[flow, at_z, at_c], zbloc.at[q])

    def ob_copy(q):
        flow, c = q // chunks, q % chunks
        at_c = pl.ds(pl.multiple_of(c * CHUNK, CHUNK), CHUNK)
        return remote(dense.at[flow, pl.ds(0, 128), at_c], o_recv.at[flow, :, at_c], ob_s.at[q], ob_r.at[q], o_peer)

    def xb_copy(q):
        flow, c = q // chunks, q % chunks
        at_c = pl.ds(pl.multiple_of(c * CHUNK, CHUNK), CHUNK)
        return remote(dense.at[flow, pl.ds(128, 64), at_c], x_recv.at[flow, :, at_c], xb_s.at[q], xb_r.at[q], x_peer)

    def send_back(q):
        for copy in zb_copies(q):
            copy.start()
        zb_local(q).start()

    def step(t, carry):
        at_t = pl.ds(pl.multiple_of((t % chunks) * CHUNK, CHUNK), CHUNK)

        @pl.when(t < chunks)
        def _():
            for copy in w_copies(t):
                copy.wait()
            for copy in w_load(t):
                copy.wait()

            @pl.when(t + 4 < chunks)
            def _():
                w_send(t + 4)

            @pl.when(t + 1 < chunks)
            def _():
                for copy in w_load(t + 1):
                    copy.start()

            def out_grad(i, carry):
                at_i = pl.ds(pl.multiple_of(i * PIECE, PIECE), PIECE)
                at_p = pl.ds(pl.multiple_of(t * CHUNK + i * PIECE, PIECE), PIECE)
                total = mm_t(small[0, 0], w_own[t % 2, 0, at_i]) + mm_t(small[1, 0], w_own[t % 2, 1, at_i])
                total += mm_t(small[0, 1], w_peer[0, at_p])
                total += mm_t(small[1, 1], w_peer[1, at_p])
                rows[0, :, at_p] = total.astype(jnp.bfloat16)
                return carry

            lax.fori_loop(0, CHUNK // PIECE, out_grad, 0)
            send_back(t)

            @pl.when(t == 0)
            def _():
                for copy in z_copies(1):
                    copy.wait()
                z_local(1).wait()
                u_load.start()

            block = rows[1, :, at_t]
            for k in range(2):
                acc[k, 0] += mm(block, w_own[t % 2, k])
                acc[k, 1] += mm(block, w_peer[k, at_t])

        @pl.when(t == chunks)
        def _():
            for k in range(2):
                gate = acc[0, k]
                hid[k] = (gate * jax.nn.sigmoid(gate) * acc[1, k]).astype(jnp.bfloat16)

        @pl.when((t >= chunks) & (t < 2 * chunks))
        def _():
            def out_rows(i, carry):
                at_p = pl.ds(pl.multiple_of((t - chunks) * CHUNK + i * PIECE, PIECE), PIECE)
                total = mm(hid[0], wd_own[:, at_p]) + mm(hid[1], wd_peer[:, at_p])
                rows[1, :, at_p] = total.astype(jnp.bfloat16)
                return carry

            lax.fori_loop(0, CHUNK // PIECE, out_rows, 0)
            send_back(t)

        @pl.when((t >= 2) & (t < 2 * chunks + 2))
        def _():
            q = t - 2
            flow = q // chunks
            at_c = pl.ds(pl.multiple_of((q % chunks) * CHUNK, CHUNK), CHUNK)
            for copy in zb_copies(q):
                copy.wait()
            zb_local(q).wait()
            block = back[flow, :, at_c]
            away = mm(comb[flow, 0, pl.ds(other, 128), 0:320], block)
            away += mm(comb[flow, 1, pl.ds(other, 128), 0:320], block)
            dense[flow, 0:128, at_c] = away.astype(jnp.bfloat16)
            ob_copy(q).start()
            keep = mm(comb[flow, 0, pl.ds(own, 128), 0:320], block)
            keep += mm(comb[flow, 1, pl.ds(own, 128), 0:320], block)
            pend[q % 3] = keep

        @pl.when((t >= 4) & (t < 2 * chunks + 4))
        def _():
            q = t - 4
            flow = q // chunks
            at_c = pl.ds(pl.multiple_of((q % chunks) * CHUNK, CHUNK), CHUNK)
            ob_copy(q).wait()
            pend[q % 3] += o_recv[flow, :, at_c].astype(jnp.float32)
            dense[flow, 128:192, at_c] = pend[q % 3, pl.ds(pl.multiple_of((1 - x) * 64, 64), 64)].astype(jnp.bfloat16)
            xb_copy(q).start()
            pend2[q % 3] = pend[q % 3, pl.ds(pl.multiple_of(x * 64, 64), 64)]

        @pl.when((t >= 6) & (t < 2 * chunks + 6))
        def _():
            q = t - 6
            flow = q // chunks
            at_c = pl.ds(pl.multiple_of((q % chunks) * CHUNK, CHUNK), CHUNK)
            xb_copy(q).wait()
            total = pend2[q % 3] + x_recv[flow, :, at_c].astype(jnp.float32)

            @pl.when(flow == 0)
            def _():
                grad[:, at_c] = total

            @pl.when(flow == 1)
            def _():
                fwd_out[:, at_c] = (fwd_out[:, at_c].astype(jnp.float32) + total).astype(jnp.bfloat16)

        @pl.when(t == 2 * chunks - 1)
        def _():
            u_load.wait()

            def norm_back(i, carry):
                at_i = pl.ds(pl.multiple_of(i * 16, 16), 16)
                u = packed[at_i].astype(jnp.float32)
                scale = lax.rsqrt(jnp.mean(u * u, axis=1, keepdims=True) + EPSILON)
                h = grad[at_i] * gains[...]
                along = jnp.mean(h * u, axis=1, keepdims=True)
                result = scale * h - u * (scale * scale * scale * along)
                bwd_out[at_i] = (bwd_out[at_i].astype(jnp.float32) + result).astype(jnp.bfloat16)
                return carry

            lax.fori_loop(0, 4, norm_back, 0)

        return carry

    lax.fori_loop(0, 2 * chunks + 6, step, 0)


def on_device(
    fwd_in, gains, gate_weight, up_weight, down_weight, fwd_routes, fwd_probs,
    bwd_grad, bwd_input, bwd_routes, bwd_probs, bwd_stash,
):
    depth = fwd_in.shape[2]
    chunks = depth // CHUNK
    hidden = gate_weight.shape[2]
    r = np.arange(384)
    goal = np.where(r < 320, (r // 80) * 2 * CAP + r % CAP + 1000 * ((r % 80) // CAP), -1000000)
    goal = jnp.asarray(goal.reshape(1, 384), jnp.float32)
    by_y = bwd_stash[0].reshape(4, 4, 2 * CAP, 2 * hidden)
    first = jnp.stack([by_y[:, 0], by_y[:, 3]], axis=1).reshape(320, 2 * hidden)
    second = jnp.stack([by_y[:, 1], by_y[:, 2]], axis=1).reshape(320, 2 * hidden)
    stash = jnp.concatenate([first, second], axis=0)
    bf, f32 = jnp.bfloat16, jnp.float32
    vmem, hbm = pl.BlockSpec(memory_space=pltpu.VMEM), pl.BlockSpec(memory_space=pl.ANY)
    dma = pltpu.SemaphoreType.DMA
    two = 2 * chunks
    scratch = [
        pltpu.VMEM((256, 128), f32),
        pltpu.VMEM((2, 256, depth), bf),
        pltpu.VMEM((320, depth), bf),
        pltpu.VMEM((2, 320, depth), bf),
        pltpu.VMEM((2, 320, depth), bf),
        pltpu.VMEM((2, 128, depth), bf),
        pltpu.VMEM((2, 64, depth), bf),
        pltpu.VMEM((hidden, depth), bf),
        pltpu.VMEM((hidden, depth), bf),
        pltpu.VMEM((2, 2, CHUNK, hidden), bf),
        pltpu.VMEM((2, depth, hidden), bf),
        pltpu.VMEM((320, 2 * hidden), bf),
        pltpu.VMEM((320, 2 * hidden), bf),
        pltpu.VMEM((2, 2, 320, hidden), f32),
        pltpu.VMEM((2, 2, 320, hidden), bf),
        pltpu.VMEM((2, 320, hidden), bf),
        pltpu.VMEM((2, 384, 256), bf),
        pltpu.VMEM((2, 2, 256, 384), bf),
        pltpu.VMEM((3, 128, CHUNK), f32),
        pltpu.VMEM((3, 64, CHUNK), f32),
        pltpu.VMEM((64, depth), f32),
        dma((2, 2)), dma((2, 2)),
        dma((3,)), dma((3,)),
        dma((2,)), dma((2,)),
        dma((2, 3)), dma((2, 3)),
        dma((2, chunks)), dma((2, chunks)),
        dma, dma,
        dma, dma,
        dma((two, 3)), dma((two, 3)),
        dma((two,)), dma((two,)),
        dma((two,)), dma((two,)),
        dma((3,)), dma((2,)), dma((2, 2)), dma((two,)),
    ]
    fwd_result, bwd_result = pl.pallas_call(
        kernel,
        out_shape=(jax.ShapeDtypeStruct((64, depth), bf), jax.ShapeDtypeStruct((64, depth), bf)),
        in_specs=[hbm, hbm, vmem, hbm, hbm, hbm, vmem, vmem, vmem, vmem, hbm, hbm, vmem],
        out_specs=(vmem, vmem),
        scratch_shapes=scratch,
        compiler_params=pltpu.CompilerParams(
            collective_id=0, has_side_effects=True, vmem_limit_bytes=63 * 1024 * 1024
        ),
        name="routed_experts",
    )(
        fwd_in[0], bwd_grad[0], gains, gate_weight[0], up_weight[0], down_weight[0],
        fwd_routes[0], fwd_probs[0], bwd_routes[0], bwd_probs[0], bwd_input[0], stash, goal,
    )
    return (fwd_result[None], bwd_result[None])


def solution(mesh):
    rows = P("section", "expert", None)
    cols = P("section", None, "expert")
    return jax.shard_map(
        on_device,
        mesh=mesh,
        in_specs=(rows, P("section", None), cols, cols, rows, rows, rows, rows, rows, rows, rows, rows),
        out_specs=(rows, rows),
        check_vma=False,
    )
```

```python
import jax
import jax.numpy as jnp
import numpy as np
from jax import lax
from jax.experimental import pallas as pl
from jax.experimental.pallas import tpu as pltpu
from jax.sharding import PartitionSpec as P

EPSILON = 1e-06
MESH = pl.DeviceIdType.MESH
CAP = 20
CHUNK = 512
PARTS = 2
PIECE = 896
NT = (((1,), (1,)), ((), ()))


def mm(a, b):
    return jnp.dot(a, b, preferred_element_type=jnp.float32)


def mm_t(a, b):
    return lax.dot_general(a, b, NT, preferred_element_type=jnp.float32)


def aligned(start, size, unit):
    return pl.ds(pl.multiple_of(start, unit), size)


def slot_keys(routes, offset):
    tokens = routes.shape[0]
    lane = lax.broadcasted_iota(jnp.int32, (tokens, 128), 1)
    first, second = routes[:, 0:1], routes[:, 1:2]
    one0 = jnp.where(first == lane, 1.0, 0.0)
    one1 = jnp.where(second == lane, 1.0, 0.0)
    row = lax.broadcasted_iota(jnp.int32, (tokens, tokens), 0)
    col = lax.broadcasted_iota(jnp.int32, (tokens, tokens), 1)
    lower = jnp.where(col < row, 1.0, 0.0).astype(jnp.bfloat16)
    before = mm(lower, (one0 + one1).astype(jnp.bfloat16))
    pos0 = jnp.sum(one0 * before, axis=1, keepdims=True)
    pos1 = jnp.sum(one1 * before, axis=1, keepdims=True)
    key0 = first.astype(jnp.float32) * CAP + pos0 + offset
    key1 = second.astype(jnp.float32) * CAP + pos1 + offset
    return key0, key1


def kernel(
    fwd_in, bwd_grad, gains, wg, wu, wd, f_routes, f_probs, b_routes, b_probs, bwd_input, stash, target,
    fwd_out, bwd_out,
    meta, scale, raw, dense, packed, rows, w_own, w_peer, wd_own, wd_peer, st, acc, psend, precv, small, hid,
    irecv, ipend, back, pend, orecv, xrecv, grad, gres, pack, comb,
    relay_s, relay_r, gres_s, gres_r, scale_s, scale_r, meta_s, meta_r, o_s, o_r, z_s, z_r, i_s, i_r,
    wt_s, wt_r, wd_s, wd_r, p_s, p_r, sm_s, sm_r, hid_s, hid_r,
    ib_s, ib_r, zb_s, zb_r, ob_s, ob_r, xb_s, xb_r, loc, zloc, zbloc,
):
    depth = gains.shape[1]
    width = depth // 2
    steps = width // CHUNK
    part = width // PARTS
    hidden = wg.shape[1]
    sec = lax.axis_index("section")
    ex = lax.axis_index("expert")
    z, y, x = ex // 8, (ex // 2) % 4, ex % 2
    half = y // 2
    cls = ((y + 1) // 2) % 2
    own = aligned(half * 128, 128, 128)
    other = aligned((1 - half) * 128, 128, 128)
    mine = aligned(half * 128 + x * 64, 64, 64)
    class_own = aligned(cls * 320, 320, 320)
    class_peer = aligned((1 - cls) * 320, 320, 320)
    cols_own = aligned(x * width, width, width)
    cols_peer = aligned((1 - x) * width, width, width)
    up, down = (sec + 1) % 4, (sec + 3) % 4

    def at(zz, yy, xx):
        return zz * 8 + yy * 2 + xx

    x_peer = (sec, at(z, y, 1 - x))
    o_peer = (sec, at(z, 3 - y, x))
    d_peer = (sec, at(z, 3 - y, 1 - x))
    i_peer = (sec, at(z, y + 1 - 2 * (y % 2), x))
    z_peers = [(sec, at((z + d) % 4, y, x)) for d in (1, 2, 3)]
    relays = [(s, at(z, y, xx)) for s in (up, down) for xx in (x, 1 - x)]

    barrier = pltpu.get_barrier_semaphore()
    partners = [x_peer, o_peer, d_peer, i_peer] + z_peers + relays
    for peer in partners:
        pl.semaphore_signal(barrier, inc=1, device_id=peer, device_id_type=MESH)
    pl.semaphore_wait(barrier, len(partners))

    def remote(src, dst, send, recv, peer):
        return pltpu.make_async_remote_copy(
            src_ref=src, dst_ref=dst, send_sem=send, recv_sem=recv, device_id=peer, device_id_type=MESH
        )

    def start(copies):
        for copy in copies:
            copy.start()

    def wait(copies):
        for copy in copies:
            copy.wait()

    def cols(k):
        return pl.ds(k * part, part)

    def relay(flow, k):
        src = (bwd_grad, fwd_in)[flow]
        copies = []
        for d, xx in enumerate((x, 1 - x)):
            dst = dense.at[0, mine, cols(k)] if flow == 0 else raw.at[aligned(x * 64, 64, 64), cols(k)]
            copies.append(remote(
                src.at[:, aligned(xx * width + k * part, part, 128)], dst,
                relay_s.at[flow, k, d], relay_r.at[flow, k, d], ((down, up)[flow], at(z, y, xx)),
            ))
        return copies

    def o_copy(flow, k):
        block = dense.at[flow, own, cols(k)]
        return remote(block, block, o_s.at[flow, k], o_r.at[flow, k], o_peer)

    def z_copies(flow, k):
        return [
            remote(
                packed.at[flow, aligned(((z + d) % 4) * 80, 80, 80), cols(k)],
                rows.at[flow, aligned(cls * 320 + z * 80, 80, 80), cols(k)],
                z_s.at[flow, k, d - 1], z_r.at[flow, k, d - 1], z_peers[d - 1],
            )
            for d in (1, 2, 3)
        ]

    def z_local(flow, k):
        return pltpu.make_async_copy(
            packed.at[flow, aligned(z * 80, 80, 80), cols(k)],
            rows.at[flow, aligned(cls * 320 + z * 80, 80, 80), cols(k)], zloc.at[flow, k],
        )

    def i_copy(flow, k):
        block = rows.at[flow, class_own, cols(k)]
        return remote(block, block, i_s.at[flow, k], i_r.at[flow, k], i_peer)

    gres_copy = remote(bwd_grad.at[:, cols_peer], gres, gres_s, gres_r, (down, at(z, y, x)))
    wd_copy = remote(wd.at[:, cols_peer], wd_peer, wd_s, wd_r, x_peer)

    def w_copies(c):
        return [
            remote(
                w.at[aligned((1 - x) * width + c * CHUNK, CHUNK, CHUNK)], w_peer.at[k, aligned(c * CHUNK, CHUNK, CHUNK)],
                wt_s.at[k, c], wt_r.at[k, c], x_peer,
            )
            for k, w in enumerate((wg, wu))
        ]

    for k in range(PARTS):
        start(relay(0, k))
    loads = [
        pltpu.make_async_copy(wd.at[:, cols_own], wd_own, loc.at[0]),
        pltpu.make_async_copy(stash, st, loc.at[1]),
        pltpu.make_async_copy(wg.at[cols_own], w_own.at[0], loc.at[2]),
        pltpu.make_async_copy(wu.at[cols_own], w_own.at[1], loc.at[3]),
    ]
    start(loads)

    for i in range(4):
        v = fwd_in[pl.ds(i * 16, 16)].astype(jnp.float32)
        r = lax.rsqrt(jnp.mean(v * v, axis=1, keepdims=True) + EPSILON)
        scale[pl.ds(128 + i * 16, 16)] = jnp.broadcast_to(r, (16, 128))
    scale_copies = [
        remote(
            scale.at[pl.ds(128, 64)], scale.at[aligned(x * 64, 64, 64)],
            scale_s.at[d], scale_r.at[d], (up, at(z, y, xx)),
        )
        for d, xx in enumerate((x, 1 - x))
    ]
    start(scale_copies)
    for k in range(PARTS):
        start(relay(1, k))

    lane = lax.broadcasted_iota(jnp.int32, (64, 128), 1)
    offset = ((half * 2 + x) * 1000).astype(jnp.float32)
    columns = []
    for routes, probs in ((b_routes, b_probs), (f_routes, f_probs)):
        key0, key1 = slot_keys(routes[...], offset)
        columns += [key0, key1, probs[:, 0:1], probs[:, 1:2]]
    value = jnp.zeros((64, 128), jnp.float32)
    for i, column in enumerate(columns):
        value = jnp.where(lane == i, column, value)
    meta[mine] = value
    meta_copies = [
        remote(meta.at[mine], meta.at[mine], meta_s.at[i], meta_r.at[i], peer)
        for i, peer in enumerate((x_peer, o_peer, d_peer))
    ]
    start(meta_copies)
    wd_copy.start()
    gres_copy.start()

    def norm(k):
        def some(i, carry):
            at_i = aligned(i * 16, 16, 16)
            v = raw[at_i, cols(k)].astype(jnp.float32)
            g = gains[:, aligned(x * width + k * part, part, 128)]
            dense[1, aligned(half * 128 + i * 16, 16, 16), cols(k)] = (v * scale[at_i, 0:1] * g).astype(jnp.bfloat16)
            return carry

        lax.fori_loop(0, 8, some, 0)

    def pack_rows(flow, k):
        o_copy(flow, k).wait()
        for j in range(part // PIECE):
            at_j = pl.ds(k * part + j * PIECE, PIECE)
            packed[flow, :, at_j] = mm(pack[flow, 0:320], dense[flow, :, at_j]).astype(jnp.bfloat16)
        start(z_copies(flow, k))
        z_local(flow, k).start()

    def pass_on(flow, k):
        wait(z_copies(flow, k))
        z_local(flow, k).wait()
        i_copy(flow, k).start()

    for k in range(PARTS):
        wait(relay(0, k))
        o_copy(0, k).start()
    bwd_out[:, cols_own] = dense[0, mine]
    wait(meta_copies)
    goal = target[...] + (half * CAP).astype(jnp.float32)
    for flow in range(2):
        base = flow * 4
        one0 = jnp.where(meta[:, base : base + 1] == goal, 1.0, 0.0)
        one1 = jnp.where(meta[:, base + 1 : base + 2] == goal, 1.0, 0.0)
        pack[flow] = jnp.transpose(one0 + one1).astype(jnp.bfloat16)
        weight = one0 * meta[:, base + 2 : base + 3] + one1 * meta[:, base + 3 : base + 4]
        high = weight.astype(jnp.bfloat16)
        comb[flow, 0] = high
        comb[flow, 1] = (weight - high.astype(jnp.float32)).astype(jnp.bfloat16)
    wait(scale_copies)
    wait(relay(1, 0))
    norm(0)
    o_copy(1, 0).start()
    pack_rows(0, 0)
    wait(relay(1, 1))
    norm(1)
    o_copy(1, 1).start()
    pack_rows(0, 1)
    pass_on(0, 0)
    start(w_copies(0))
    pack_rows(1, 0)
    pass_on(0, 1)
    start(w_copies(1))
    pack_rows(1, 1)
    pass_on(1, 0)
    pass_on(1, 1)
    start(w_copies(2))

    wait(loads)
    wd_copy.wait()
    acc[...] = jnp.zeros_like(acc)
    for k in range(PARTS):
        i_copy(0, k).wait()

        def hid_grad(j, carry):
            at_j = aligned(k * part + j * PIECE, PIECE, 128)
            block = rows[0, :, at_j]
            acc[0, 0] += mm_t(block, wd_own[:, at_j])
            acc[0, 1] += mm_t(block, wd_peer[:, at_j])
            return carry

        lax.fori_loop(0, part // PIECE, hid_grad, 0)

    def p_copy(i):
        return remote(psend.at[i], precv.at[i], p_s.at[i], p_r.at[i], x_peer)

    psend[0] = acc[0, 1].astype(jnp.bfloat16)
    p_copy(0).start()
    p_copy(0).wait()

    def gates(i, carry):
        at_i = aligned(i * 160, 160, 160)
        a = st[at_i, 0:hidden].astype(jnp.float32)
        b = st[at_i, hidden : 2 * hidden].astype(jnp.float32)
        sig = jax.nn.sigmoid(a)
        g = acc[0, 0, at_i] + precv[0, at_i].astype(jnp.float32)
        small[0, 0, at_i] = (g * b * sig * (1.0 + a * (1.0 - sig))).astype(jnp.bfloat16)
        small[1, 0, at_i] = (g * a * sig).astype(jnp.bfloat16)
        return carry

    lax.fori_loop(0, 4, gates, 0)
    small_copies = [remote(small.at[k, 0], small.at[k, 1], sm_s.at[k], sm_r.at[k], x_peer) for k in range(2)]
    start(small_copies)
    start(w_copies(3))
    acc[...] = jnp.zeros_like(acc)
    wait(small_copies)
    hid_copy = remote(hid.at[0], hid.at[1], hid_s, hid_r, x_peer)

    def place(q):
        return q // steps, aligned((q % steps) * CHUNK, CHUNK, CHUNK)

    def ib_copy(q):
        flow, at_c = place(q)
        return remote(rows.at[flow, class_peer, at_c], irecv.at[flow, :, at_c], ib_s.at[q], ib_r.at[q], i_peer)

    def zb_copies(q):
        flow, at_c = place(q)
        return [
            remote(
                rows.at[flow, aligned(cls * 320 + ((z + d) % 4) * 80, 80, 80), at_c],
                back.at[flow, aligned(z * 80, 80, 80), at_c],
                zb_s.at[q, d - 1], zb_r.at[q, d - 1], z_peers[d - 1],
            )
            for d in (1, 2, 3)
        ]

    def zb_local(q):
        flow, at_c = place(q)
        return pltpu.make_async_copy(
            rows.at[flow, aligned(cls * 320 + z * 80, 80, 80), at_c],
            back.at[flow, aligned(z * 80, 80, 80), at_c], zbloc.at[q],
        )

    def ob_copy(q):
        flow, at_c = place(q)
        return remote(dense.at[flow, pl.ds(0, 128), at_c], orecv.at[flow, :, at_c], ob_s.at[q], ob_r.at[q], o_peer)

    def xb_copy(q):
        flow, at_c = place(q)
        return remote(dense.at[flow, pl.ds(128, 64), at_c], xrecv.at[flow, :, at_c], xb_s.at[q], xb_r.at[q], x_peer)

    def step(t, carry):
        at_t = aligned((t % (steps + 1)) * CHUNK, CHUNK, CHUNK)

        @pl.when(t < steps)
        def _():
            wait(w_copies(t))

            @pl.when(t + 4 < steps)
            def _():
                start(w_copies(t + 4))

            def out_grad(at_rows):
                total = mm_t(small[0, 0, at_rows], w_own[0, at_t]) + mm_t(small[1, 0, at_rows], w_own[1, at_t])
                total += mm_t(small[0, 1, at_rows], w_peer[0, at_t])
                total += mm_t(small[1, 1, at_rows], w_peer[1, at_t])
                return total

            rows[0, class_peer, at_t] = out_grad(class_peer).astype(jnp.bfloat16)
            ib_copy(t).start()
            ipend[t % 3] = out_grad(class_own)

            @pl.when(t == 0)
            def _():
                for k in range(PARTS):
                    i_copy(1, k).wait()

            block = rows[1, :, at_t]
            for k in range(2):
                acc[k, 0] += mm(block, w_own[k, at_t])
                acc[k, 1] += mm(block, w_peer[k, at_t])

            @pl.when(t == steps - 1)
            def _():
                for k in range(2):
                    psend[1 + k] = acc[k, 1].astype(jnp.bfloat16)
                    p_copy(1 + k).start()

        @pl.when(t == steps)
        def _():
            for k in range(2):
                p_copy(1 + k).wait()

            def gated(i, carry):
                at_i = aligned(i * 160, 160, 160)
                gate = acc[0, 0, at_i] + precv[1, at_i].astype(jnp.float32)
                upper = acc[1, 0, at_i] + precv[2, at_i].astype(jnp.float32)
                hid[0, at_i] = (gate * jax.nn.sigmoid(gate) * upper).astype(jnp.bfloat16)
                return carry

            lax.fori_loop(0, 4, gated, 0)
            hid_copy.start()

        @pl.when((t > steps) & (t < 2 * steps + 1))
        def _():
            @pl.when(t == steps + 1)
            def _():
                hid_copy.wait()

            def out_rows(at_rows):
                return mm(hid[0, at_rows], wd_own[:, at_t]) + mm(hid[1, at_rows], wd_peer[:, at_t])

            rows[1, class_peer, at_t] = out_rows(class_peer).astype(jnp.bfloat16)
            ib_copy(t - 1).start()
            ipend[t % 3] = out_rows(class_own)

        def lagging(lag):
            s = t - lag
            return s, s - s // (steps + 1), (s >= 0) & (s < 2 * steps + 1) & (s != steps)

        s2, q2, due2 = lagging(2)

        @pl.when(due2)
        def _():
            flow, at_c = place(q2)
            ib_copy(q2).wait()
            total = ipend[s2 % 3] + irecv[flow, :, at_c].astype(jnp.float32)
            rows[flow, class_own, at_c] = total.astype(jnp.bfloat16)
            start(zb_copies(q2))
            zb_local(q2).start()

        s4, q4, due4 = lagging(4)

        @pl.when(due4)
        def _():
            flow, at_c = place(q4)
            wait(zb_copies(q4))
            zb_local(q4).wait()
            block = back[flow, :, at_c]
            away = mm(comb[flow, 0, other, 0:320], block) + mm(comb[flow, 1, other, 0:320], block)
            dense[flow, 0:128, at_c] = away.astype(jnp.bfloat16)
            ob_copy(q4).start()
            pend[s4 % 3] = mm(comb[flow, 0, own, 0:320], block) + mm(comb[flow, 1, own, 0:320], block)

        s6, q6, due6 = lagging(6)

        @pl.when(due6)
        def _():
            flow, at_c = place(q6)
            c = (q6 % steps) * CHUNK
            rows_mine, rows_peer = aligned(x * 64, 64, 64), aligned((1 - x) * 64, 64, 64)
            ob_copy(q6).wait()
            total = pend[s6 % 3] + orecv[flow, :, at_c].astype(jnp.float32)
            at_d = aligned(x * width + c, CHUNK, CHUNK)

            @pl.when(flow == 0)
            def _():
                pend[s6 % 3] = total
                grad[:, at_d] = pend[s6 % 3, rows_mine]

            @pl.when(flow == 1)
            def _():
                pend[s6 % 3] = total + raw[:, at_c].astype(jnp.float32)
                fwd_out[:, at_d] = pend[s6 % 3, rows_mine].astype(jnp.bfloat16)

            dense[flow, 128:192, at_c] = pend[s6 % 3, rows_peer].astype(jnp.bfloat16)
            xb_copy(q6).start()

        _, q8, due8 = lagging(8)

        @pl.when(due8)
        def _():
            flow, at_c = place(q8)
            at_d = aligned((1 - x) * width + (q8 % steps) * CHUNK, CHUNK, CHUNK)
            xb_copy(q8).wait()

            @pl.when(flow == 0)
            def _():
                grad[:, at_d] = xrecv[0, :, at_c].astype(jnp.float32)

            @pl.when(flow == 1)
            def _():
                fwd_out[:, at_d] = xrecv[1, :, at_c]

        @pl.when(t == 2 * steps + 1)
        def _():
            gres_copy.wait()
            bwd_out[:, cols_peer] = gres[...]

            def norm_back(i, carry):
                at_i = aligned(i * 16, 16, 16)
                u = bwd_input[at_i].astype(jnp.float32)
                r = lax.rsqrt(jnp.mean(u * u, axis=1, keepdims=True) + EPSILON)
                h = grad[at_i] * gains[...]
                along = jnp.mean(h * u, axis=1, keepdims=True)
                result = r * h - u * (r * r * r * along)
                bwd_out[at_i] = (bwd_out[at_i].astype(jnp.float32) + result).astype(jnp.bfloat16)
                return carry

            lax.fori_loop(0, 4, norm_back, 0)

        return carry

    lax.fori_loop(0, 2 * steps + 9, step, 0)


def on_device(
    fwd_in, gains, gate_weight, up_weight, down_weight, fwd_routes, fwd_probs,
    bwd_grad, bwd_input, bwd_routes, bwd_probs, bwd_stash,
):
    depth = fwd_in.shape[2]
    width = depth // 2
    hidden = gate_weight.shape[2]
    r = np.arange(384)
    goal = np.where(r < 320, (r // 80) * 2 * CAP + r % CAP + 1000 * ((r % 80) // CAP), -1000000)
    goal = jnp.asarray(goal.reshape(1, 384), jnp.float32)
    by_y = bwd_stash[0].reshape(4, 4, 2 * CAP, 2 * hidden)
    first = jnp.stack([by_y[:, 0], by_y[:, 3]], axis=1).reshape(320, 2 * hidden)
    second = jnp.stack([by_y[:, 1], by_y[:, 2]], axis=1).reshape(320, 2 * hidden)
    stash = jnp.concatenate([first, second], axis=0)
    bf, f32 = jnp.bfloat16, jnp.float32
    vmem, hbm = pl.BlockSpec(memory_space=pltpu.VMEM), pl.BlockSpec(memory_space=pl.ANY)
    dma = pltpu.SemaphoreType.DMA
    steps = width // CHUNK
    two = 2 * steps
    scratch = [
        pltpu.VMEM((256, 128), f32),
        pltpu.VMEM((192, 128), f32),
        pltpu.VMEM((128, width), bf),
        pltpu.VMEM((2, 256, width), bf),
        pltpu.VMEM((2, 320, width), bf),
        pltpu.VMEM((2, 640, width), bf),
        pltpu.VMEM((2, width, hidden), bf),
        pltpu.VMEM((2, width, hidden), bf),
        pltpu.VMEM((hidden, width), bf),
        pltpu.VMEM((hidden, width), bf),
        pltpu.VMEM((640, 2 * hidden), bf),
        pltpu.VMEM((2, 2, 640, hidden), f32),
        pltpu.VMEM((3, 640, hidden), bf),
        pltpu.VMEM((3, 640, hidden), bf),
        pltpu.VMEM((2, 2, 640, hidden), bf),
        pltpu.VMEM((2, 640, hidden), bf),
        pltpu.VMEM((2, 320, width), bf),
        pltpu.VMEM((3, 320, CHUNK), f32),
        pltpu.VMEM((2, 320, width), bf),
        pltpu.VMEM((3, 128, CHUNK), f32),
        pltpu.VMEM((2, 128, width), bf),
        pltpu.VMEM((2, 64, width), bf),
        pltpu.VMEM((64, depth), f32),
        pltpu.VMEM((64, width), bf),
        pltpu.VMEM((2, 384, 256), bf),
        pltpu.VMEM((2, 2, 256, 384), bf),
        dma((2, PARTS, 2)), dma((2, PARTS, 2)),
        dma, dma,
        dma((2,)), dma((2,)),
        dma((3,)), dma((3,)),
        dma((2, PARTS)), dma((2, PARTS)),
        dma((2, PARTS, 3)), dma((2, PARTS, 3)),
        dma((2, PARTS)), dma((2, PARTS)),
        dma((2, steps)), dma((2, steps)),
        dma, dma,
        dma((3,)), dma((3,)),
        dma((2,)), dma((2,)),
        dma, dma,
        dma((two,)), dma((two,)),
        dma((two, 3)), dma((two, 3)),
        dma((two,)), dma((two,)),
        dma((two,)), dma((two,)),
        dma((4,)), dma((2, PARTS)), dma((two,)),
    ]
    fwd_result, bwd_result = pl.pallas_call(
        kernel,
        out_shape=(jax.ShapeDtypeStruct((64, depth), bf), jax.ShapeDtypeStruct((64, depth), bf)),
        in_specs=[vmem, hbm, vmem, hbm, hbm, hbm, vmem, vmem, vmem, vmem, vmem, hbm, vmem],
        out_specs=(vmem, vmem),
        scratch_shapes=scratch,
        compiler_params=pltpu.CompilerParams(
            collective_id=0, has_side_effects=True, vmem_limit_bytes=63 * 1024 * 1024
        ),
        name="routed_experts",
    )(
        fwd_in[0], bwd_grad[0], gains, gate_weight[0], up_weight[0], down_weight[0],
        fwd_routes[0], fwd_probs[0], bwd_routes[0], bwd_probs[0], bwd_input[0], stash, goal,
    )
    return (fwd_result[None], bwd_result[None])


def solution(mesh):
    rows = P("section", "expert", None)
    cols = P("section", None, "expert")
    return jax.shard_map(
        on_device,
        mesh=mesh,
        in_specs=(rows, P("section", None), cols, cols, rows, rows, rows, rows, rows, rows, rows, rows),
        out_specs=(rows, rows),
        check_vma=False,
    )
```

```python
import jax
import jax.numpy as jnp
import numpy as np
from jax import lax
from jax.experimental import pallas as pl
from jax.experimental.pallas import tpu as pltpu
from jax.sharding import PartitionSpec as P

EPSILON = 1e-06
MESH = pl.DeviceIdType.MESH
CAP = 20
EARLY = 4
RING = 4
CHUNK = 512
PARTS = 4
PIECE = 896
NT = (((1,), (1,)), ((), ()))


def mm(a, b):
    return jnp.dot(a, b, preferred_element_type=jnp.float32)


def mm_t(a, b):
    return lax.dot_general(a, b, NT, preferred_element_type=jnp.float32)


def aligned(start, size, unit):
    return pl.ds(pl.multiple_of(start, unit), size)


def slot_keys(first, second, offset):
    tokens = first.shape[1]
    expert = lax.broadcasted_iota(jnp.int32, (8, tokens), 0).astype(jnp.float32)
    one0 = jnp.where(first == expert, 1.0, 0.0)
    one1 = jnp.where(second == expert, 1.0, 0.0)
    row = lax.broadcasted_iota(jnp.int32, (tokens, tokens), 0)
    col = lax.broadcasted_iota(jnp.int32, (tokens, tokens), 1)
    earlier = jnp.where(row < col, 1.0, 0.0).astype(jnp.bfloat16)
    before = mm((one0 + one1).astype(jnp.bfloat16), earlier)
    pos0 = jnp.sum(one0 * before, axis=0, keepdims=True)
    pos1 = jnp.sum(one1 * before, axis=0, keepdims=True)
    return first * CAP + pos0 + offset, second * CAP + pos1 + offset


def kernel(
    fwd_in, bwd_grad, gains, wg, wu, wd, f_routes, f_probs, b_routes, b_probs, bwd_input, stash, target,
    fwd_out, bwd_out,
    told, meta, scales, scale, raw, dense, packed, rows, w_own, w_peer, wd_own, wd_peer, st, acc, psend, precv, small, hid,
    irecv, ipend, back, back2, pend, pend2, orecv, orecv2, xrecv, grad, gres, pack, comb,
    relay_s, relay_r, gres_s, gres_r, scale_s, scale_r, meta_s, meta_r, o_s, o_r, z_s, z_r, i_s, i_r,
    wt_s, wt_r, wd_s, wd_r, p_s, p_r, sm_s, sm_r, hid_s, hid_r,
    ib_s, ib_r, zz_s, zz_r, zzloc, zb_s, zb_r, ob_s, ob_r, xb_s, xb_r, loc, zloc, zbloc,
):
    depth = gains.shape[1]
    width = depth // 2
    steps = width // CHUNK
    part = width // PARTS
    hidden = wg.shape[1]
    sec = lax.axis_index("section")
    ex = lax.axis_index("expert")
    z, y, x = ex // 8, (ex // 2) % 4, ex % 2
    half = y // 2
    cls = ((y + 1) // 2) % 2
    own = aligned(half * 128, 128, 128)
    other = aligned((1 - half) * 128, 128, 128)
    mine = aligned(half * 128 + x * 64, 64, 64)
    class_own = aligned(cls * 320, 320, 320)
    class_peer = aligned((1 - cls) * 320, 320, 320)
    cols_own = aligned(x * width, width, width)
    cols_peer = aligned((1 - x) * width, width, width)
    up, down = (sec + 1) % 4, (sec + 3) % 4

    def at(zz, yy, xx):
        return zz * 8 + yy * 2 + xx

    x_peer = (sec, at(z, y, 1 - x))
    o_peer = (sec, at(z, 3 - y, x))
    d_peer = (sec, at(z, 3 - y, 1 - x))
    i_peer = (sec, at(z, y + 1 - 2 * (y % 2), x))
    c_peers = [(sec, at(z, yy, xx)) for yy in (y + 1 - 2 * (y % 2), 2 + y % 2 - 2 * half) for xx in (x, 1 - x)]
    z_peers = [(sec, at((z + d) % 4, y, x)) for d in (1, 2, 3)]
    relays = [(s, at(z, y, xx)) for s in (up, down) for xx in (x, 1 - x)]

    barrier = pltpu.get_barrier_semaphore()
    partners = [x_peer, o_peer, d_peer] + c_peers + z_peers + relays
    for peer in partners:
        pl.semaphore_signal(barrier, inc=1, device_id=peer, device_id_type=MESH)
    pl.semaphore_wait(barrier, len(partners))

    def remote(src, dst, send, recv, peer):
        return pltpu.make_async_remote_copy(
            src_ref=src, dst_ref=dst, send_sem=send, recv_sem=recv, device_id=peer, device_id_type=MESH
        )

    def start(copies):
        for copy in copies:
            copy.start()

    def wait(copies):
        for copy in copies:
            copy.wait()

    def cols(k):
        return pl.ds(k * part, part)

    def relay(flow, k):
        src = (bwd_grad, fwd_in)[flow]
        copies = []
        for d, xx in enumerate((x, 1 - x)):
            dst = dense.at[0, mine, cols(k)] if flow == 0 else raw.at[aligned(x * 64, 64, 64), cols(k)]
            copies.append(remote(
                src.at[:, aligned(xx * width + k * part, part, 128)], dst,
                relay_s.at[flow, k, d], relay_r.at[flow, k, d], ((down, up)[flow], at(z, y, xx)),
            ))
        return copies

    def o_copy(flow, k):
        block = dense.at[flow, own, cols(k)]
        return remote(block, block, o_s.at[flow, k], o_r.at[flow, k], o_peer)

    def z_copies(flow, k):
        return [
            remote(
                packed.at[flow, aligned(((z + d) % 4) * 80, 80, 80), cols(k)],
                rows.at[flow, aligned(cls * 320 + z * 80, 80, 80), cols(k)],
                z_s.at[flow, k, d - 1], z_r.at[flow, k, d - 1], z_peers[d - 1],
            )
            for d in (1, 2, 3)
        ]

    def z_local(flow, k):
        return pltpu.make_async_copy(
            packed.at[flow, aligned(z * 80, 80, 80), cols(k)],
            rows.at[flow, aligned(cls * 320 + z * 80, 80, 80), cols(k)], zloc.at[flow, k],
        )

    def i_copy(flow, k):
        block = rows.at[flow, class_own, cols(k)]
        return remote(block, block, i_s.at[flow, k], i_r.at[flow, k], i_peer)

    gres_copy = remote(bwd_grad.at[:, cols_peer], gres, gres_s, gres_r, (down, at(z, y, x)))
    wd_copy = remote(wd.at[:, cols_peer], wd_peer, wd_s, wd_r, x_peer)

    def w_copies(c):
        return [
            remote(
                w.at[aligned((1 - x) * width + c * CHUNK, CHUNK, CHUNK)], w_peer.at[k, aligned(c * CHUNK, CHUNK, CHUNK)],
                wt_s.at[k, c], wt_r.at[k, c], x_peer,
            )
            for k, w in enumerate((wg, wu))
        ]

    for k in range(PARTS):
        start(relay(0, k))
    loads = [
        pltpu.make_async_copy(wd.at[:, cols_own], wd_own, loc.at[0]),
        pltpu.make_async_copy(stash.at[:, 0:hidden], small.at[0, 0], loc.at[1]),
        pltpu.make_async_copy(stash.at[:, hidden : 2 * hidden], small.at[1, 0], loc.at[4]),
        pltpu.make_async_copy(wg.at[cols_own], w_own.at[0], loc.at[2]),
        pltpu.make_async_copy(wu.at[cols_own], w_own.at[1], loc.at[3]),
    ]
    start(loads)

    offset = ((half * 2 + x) * 1000).astype(jnp.float32)
    lines = []
    for routes, probs in ((b_routes, b_probs), (f_routes, f_probs)):
        chosen = routes[...].astype(jnp.float32)
        lines += [*slot_keys(chosen[0:1], chosen[1:2], offset), probs[...]]
    lines = jnp.concatenate(lines, axis=0)
    my_lines = aligned((cls * 4 + half * 2 + x) * 8, 8, 8)
    told[my_lines] = jnp.concatenate([lines, jnp.zeros((8, 64), jnp.float32)], axis=1)
    meta_copies = [
        remote(told.at[my_lines], told.at[my_lines], meta_s.at[i], meta_r.at[i], peer)
        for i, peer in enumerate([x_peer, o_peer, d_peer] + c_peers)
    ]
    start(meta_copies)

    for i in range(4):
        v = fwd_in[pl.ds(i * 16, 16)].astype(jnp.float32)
        r = lax.rsqrt(jnp.mean(v * v, axis=1, keepdims=True) + EPSILON)
        scale[pl.ds(i * 16, 16)] = jnp.broadcast_to(r, (16, 128))
    turned = jnp.transpose(jnp.concatenate([scale[0:64], jnp.zeros((64, 128), jnp.float32)], axis=0))
    scales[16:24] = turned[0:8]
    scale_copies = [
        remote(
            scales.at[16:24], scales.at[aligned(x * 8, 8, 8)], scale_s.at[d], scale_r.at[d], (up, at(z, y, xx))
        )
        for d, xx in enumerate((x, 1 - x))
    ]
    start(scale_copies)
    for k in range(PARTS):
        start(relay(1, k))
    wd_copy.start()

    def norm(k):
        def some(i, carry):
            at_i = aligned(i * 16, 16, 16)
            v = raw[at_i, cols(k)].astype(jnp.float32)
            g = gains[:, aligned(x * width + k * part, part, 128)]
            dense[1, aligned(half * 128 + i * 16, 16, 16), cols(k)] = (v * scale[at_i, 0:1] * g).astype(jnp.bfloat16)
            return carry

        lax.fori_loop(0, 8, some, 0)

    def pack_rows(flow, k):
        o_copy(flow, k).wait()
        for j in range(part // PIECE):
            at_j = pl.ds(k * part + j * PIECE, PIECE)
            packed[flow, :, at_j] = mm(pack[flow, 0:320], dense[flow, :, at_j]).astype(jnp.bfloat16)
        start(z_copies(flow, k))
        z_local(flow, k).start()

    def pass_on(flow, k):
        wait(z_copies(flow, k))
        z_local(flow, k).wait()
        i_copy(flow, k).start()

    def relayed(flow, k):
        wait(relay(flow, k))
        if flow == 1:
            norm(k)
        o_copy(flow, k).start()

    goal = target[...] + (half * CAP).astype(jnp.float32)

    def column(group, i):
        return meta[aligned(group * 256, 256, 256), i : i + 1]

    def matches(group, i):
        return jnp.where(column(group, i) == goal, 1.0, 0.0)

    def build_pack(flow):
        pack[flow] = jnp.transpose(matches(cls, flow * 4) + matches(cls, flow * 4 + 1)).astype(jnp.bfloat16)

    def build_comb(at_i, group, base):
        weight = matches(group, base) * column(group, base + 2) + matches(group, base + 1) * column(group, base + 3)
        high = weight.astype(jnp.bfloat16)
        comb[at_i, 0] = high
        comb[at_i, 1] = (weight - high.astype(jnp.float32)).astype(jnp.bfloat16)

    relayed(0, 0)
    relayed(0, 1)
    wait(meta_copies)
    turned = jnp.transpose(jnp.concatenate([told[...], jnp.zeros((64, 128), jnp.float32)], axis=0))
    for i in range(8):
        meta[i * 64 : i * 64 + 64, 0:8] = turned[0:64, i * 8 : i * 8 + 8]
    build_pack(0)
    relayed(0, 2)
    pack_rows(0, 0)
    relayed(0, 3)
    pack_rows(0, 1)
    wait(scale_copies)
    both = jnp.concatenate([scales[0:1, 0:64], scales[8:9, 0:64]], axis=1)
    scale[...] = jnp.transpose(jnp.broadcast_to(both, (128, 128)))
    relayed(1, 0)
    pass_on(0, 0)
    pack_rows(0, 2)
    relayed(1, 1)
    pass_on(0, 1)
    pack_rows(0, 3)
    relayed(1, 2)
    build_pack(1)
    pass_on(0, 2)
    relayed(1, 3)
    start(w_copies(0))
    pass_on(0, 3)
    pack_rows(1, 0)
    pack_rows(1, 1)
    start(w_copies(1))
    pack_rows(1, 2)
    pass_on(1, 0)
    pack_rows(1, 3)
    pass_on(1, 1)
    start(w_copies(2))
    pass_on(1, 2)
    pass_on(1, 3)
    bwd_out[:, cols_own] = dense[0, mine]
    build_comb(0, cls, 0)
    build_comb(1, cls, 4)
    build_comb(2, 1 - cls, 4)
    wait(loads)
    for c, pair in enumerate(((0, 3), (1, 2))):
        for zz in range(4):
            for k in range(2):
                blocks = [small[k, 0, zz * 160 + yy * 40 : zz * 160 + yy * 40 + 40].astype(jnp.float32) for yy in pair]
                at_block = pl.ds(c * 320 + zz * 80, 80)
                st[at_block, k * hidden : (k + 1) * hidden] = jnp.concatenate(blocks, axis=0).astype(jnp.bfloat16)
    u_loads = [
        pltpu.make_async_copy(
            bwd_input.at[:, pl.ds(k * width, width)], packed.at[0, pl.ds(128 + k * 64, 64)], loc.at[5 + k]
        )
        for k in range(2)
    ]
    start(u_loads)

    wd_copy.wait()
    acc[...] = jnp.zeros_like(acc)
    for k in range(PARTS):
        i_copy(0, k).wait()

        def hid_grad(j, carry):
            at_j = aligned(k * part + j * PIECE, PIECE, 128)
            block = rows[0, :, at_j]
            acc[0, 0] += mm_t(block, wd_own[:, at_j])
            acc[0, 1] += mm_t(block, wd_peer[:, at_j])
            return carry

        lax.fori_loop(0, part // PIECE, hid_grad, 0)

    classes = (class_peer, class_own)

    def p_copy(i, h):
        return remote(psend.at[i, classes[h]], precv.at[i, classes[h]], p_s.at[i, h], p_r.at[i, h], x_peer)

    psend[0] = acc[0, 1].astype(jnp.bfloat16)
    for h in range(2):
        p_copy(0, h).start()
    for h in range(2):
        p_copy(0, h).wait()

    def gates(i, carry):
        at_i = aligned(i * 160, 160, 160)
        a = st[at_i, 0:hidden].astype(jnp.float32)
        b = st[at_i, hidden : 2 * hidden].astype(jnp.float32)
        sig = jax.nn.sigmoid(a)
        g = acc[0, 0, at_i] + precv[0, at_i].astype(jnp.float32)
        small[0, 0, at_i] = (g * b * sig * (1.0 + a * (1.0 - sig))).astype(jnp.bfloat16)
        small[1, 0, at_i] = (g * a * sig).astype(jnp.bfloat16)
        return carry

    lax.fori_loop(0, 4, gates, 0)
    small_copies = [remote(small.at[k, 0], small.at[k, 1], sm_s.at[k], sm_r.at[k], x_peer) for k in range(2)]
    start(small_copies)
    start(w_copies(3))
    acc[...] = jnp.zeros_like(acc)
    wait(small_copies)

    def hid_copy(h):
        return remote(hid.at[0, classes[h]], hid.at[1, classes[h]], hid_s.at[h], hid_r.at[h], x_peer)


    def plain(q):
        return (q < steps) | ((q - steps) % 2 == 0)

    def place(q):
        return q // steps, aligned((q % steps) * CHUNK, CHUNK, CHUNK)

    def ib_copy(q):
        flow, at_c = place(q)
        return remote(rows.at[flow, class_peer, at_c], irecv.at[flow, :, at_c], ib_s.at[q], ib_r.at[q], i_peer)

    def zb_copies(q):
        flow, at_c = place(q)
        return [
            remote(
                rows.at[flow, aligned(cls * 320 + ((z + d) % 4) * 80, 80, 80), at_c],
                back.at[flow, aligned(z * 80, 80, 80), at_c],
                zb_s.at[q, d - 1], zb_r.at[q, d - 1], z_peers[d - 1],
            )
            for d in (1, 2, 3)
        ]

    def zb_local(q):
        flow, at_c = place(q)
        return pltpu.make_async_copy(
            rows.at[flow, aligned(cls * 320 + z * 80, 80, 80), at_c],
            back.at[flow, aligned(z * 80, 80, 80), at_c], zbloc.at[q],
        )

    def ob_copy(q):
        flow, at_c = place(q)
        return remote(dense.at[flow, pl.ds(0, 128), at_c], orecv.at[flow, :, at_c], ob_s.at[q], ob_r.at[q], o_peer)

    def xb_copy(q):
        flow, at_c = place(q)
        return remote(dense.at[flow, pl.ds(128, 64), at_c], xrecv.at[flow, :, at_c], xb_s.at[q], xb_r.at[q], x_peer)

    def gate_sums(c):
        at_c = aligned(c * CHUNK, CHUNK, CHUNK)
        block = rows[1, :, at_c]
        for k in range(2):
            acc[k, 0] += mm(block, w_own[k, at_c])
            acc[k, 1] += mm(block, w_peer[k, at_c])

    def out_grad(c, carry):
        at_c = aligned(c * CHUNK, CHUNK, CHUNK)
        wait(w_copies(c))

        @pl.when(c + 4 < steps)
        def _():
            start(w_copies(c + 4))

        def total(at_rows):
            value = mm_t(small[0, 0, at_rows], w_own[0, at_c]) + mm_t(small[1, 0, at_rows], w_own[1, at_c])
            value += mm_t(small[0, 1, at_rows], w_peer[0, at_c])
            value += mm_t(small[1, 1, at_rows], w_peer[1, at_c])
            return value

        rows[0, class_peer, at_c] = total(class_peer).astype(jnp.bfloat16)
        ib_copy(c).start()
        ipend[c] = total(class_own)

        @pl.when(c == EARLY)
        def _():
            for k in range(PARTS):
                i_copy(1, k).wait()

            def earlier(j, carry):
                gate_sums(j)
                return carry

            lax.fori_loop(0, EARLY, earlier, 0)

        @pl.when(c >= EARLY)
        def _():
            gate_sums(c)

        return carry

    def out_rows(c):
        at_c = aligned(c * CHUNK, CHUNK, CHUNK)

        def total(at_rows):
            return mm(hid[0, at_rows], wd_own[:, at_c]) + mm(hid[1, at_rows], wd_peer[:, at_c])

        rows[1, class_peer, at_c] = total(class_peer).astype(jnp.bfloat16)

        @pl.when(c % 2 == 0)
        def _():
            ib_copy(steps + c).start()

        @pl.when(c % 2 == 1)
        def _():
            for j in range(3):
                zz_copy(c // 2, 0, j).start()
            zz_local(c // 2, 0).start()

        @pl.when(c == 0)
        def _():
            hid_copy(1).wait()

        @pl.when(c % 2 == 0)
        def _():
            ipend[c] = total(class_own)

        @pl.when(c % 2 == 1)
        def _():
            rows[1, class_own, at_c] = total(class_own).astype(jnp.bfloat16)
            for j in range(3):
                zz_copy(c // 2, 1, j).start()
            zz_local(c // 2, 1).start()

    def zz_copy(b, h, j):
        at_c = aligned((2 * b + 1) * CHUNK, CHUNK, CHUNK)
        src_row = ((1 - cls) if h == 0 else cls) * 320 + ((z + j + 1) % 4) * 80
        at_z = aligned(z * 80, 80, 80)
        dst = back2.at[at_z, aligned(b * CHUNK, CHUNK, CHUNK)] if h == 0 else back.at[1, at_z, at_c]
        return remote(
            rows.at[1, aligned(src_row, 80, 80), at_c], dst, zz_s.at[b, h, j], zz_r.at[b, h, j], z_peers[j]
        )

    def zz_local(b, h):
        at_c = aligned((2 * b + 1) * CHUNK, CHUNK, CHUNK)
        src_row = ((1 - cls) if h == 0 else cls) * 320 + z * 80
        at_z = aligned(z * 80, 80, 80)
        dst = back2.at[at_z, aligned(b * CHUNK, CHUNK, CHUNK)] if h == 0 else back.at[1, at_z, at_c]
        return pltpu.make_async_copy(rows.at[1, aligned(src_row, 80, 80), at_c], dst, zzloc.at[b, h])

    def oo_copy(q):
        _, at_c = place(q)
        b = (q - steps) // 2
        return remote(
            packed.at[1, pl.ds(0, 256), at_c], orecv2.at[:, aligned(b * CHUNK, CHUNK, CHUNK)],
            ob_s.at[q], ob_r.at[q], o_peer,
        )

    def ii_copy(q):
        _, at_c = place(q)
        return remote(packed.at[0, pl.ds(0, 128), at_c], irecv.at[1, pl.ds(0, 128), at_c], ib_s.at[q], ib_r.at[q], i_peer)

    def combine_all(q):
        _, at_c = place(q)
        b = (q - steps) // 2
        for h in range(2):
            for j in range(3):
                zz_copy(b, h, j).wait()
            zz_local(b, h).wait()
            i = 2 - h
            block = back2[:, aligned(b * CHUNK, CHUNK, CHUNK)] if h == 0 else back[1, :, at_c]
            away = mm(comb[i, 0, other, 0:320], block) + mm(comb[i, 1, other, 0:320], block)
            at_group = aligned(((1 - cls) if h == 0 else cls) * 128, 128, 128)
            packed[1, at_group, at_c] = away.astype(jnp.bfloat16)
            pend2[b % 2, h] = mm(comb[i, 0, own, 0:320], block) + mm(comb[i, 1, own, 0:320], block)
        oo_copy(q).start()

    def add_outer_all(q):
        _, at_c = place(q)
        b = (q - steps) // 2
        at_b = aligned(b * CHUNK, CHUNK, CHUNK)
        oo_copy(q).wait()
        peers = pend2[b % 2, 0] + orecv2[aligned((1 - cls) * 128, 128, 128), at_b].astype(jnp.float32)
        packed[0, 0:128, at_c] = peers.astype(jnp.bfloat16)
        ii_copy(q).start()
        pend[q % RING] = pend2[b % 2, 1] + orecv2[aligned(cls * 128, 128, 128), at_b].astype(jnp.float32)

    def add_pair(q):
        flow, at_c = place(q)
        ib_copy(q).wait()
        total = ipend[q % steps] + irecv[flow, :, at_c].astype(jnp.float32)
        rows[flow, class_own, at_c] = total.astype(jnp.bfloat16)
        start(zb_copies(q))
        zb_local(q).start()

    def combine(q):
        flow, at_c = place(q)
        wait(zb_copies(q))
        zb_local(q).wait()
        block = back[flow, :, at_c]
        away = mm(comb[flow, 0, other, 0:320], block) + mm(comb[flow, 1, other, 0:320], block)
        dense[flow, 0:128, at_c] = away.astype(jnp.bfloat16)
        ob_copy(q).start()
        pend[q % RING] = mm(comb[flow, 0, own, 0:320], block) + mm(comb[flow, 1, own, 0:320], block)

    def add_outer(q):
        flow, at_c = place(q)
        slot = q % RING
        rows_mine, rows_peer = aligned(x * 64, 64, 64), aligned((1 - x) * 64, 64, 64)

        @pl.when(plain(q))
        def _():
            ob_copy(q).wait()
            pend[slot] += orecv[flow, :, at_c].astype(jnp.float32)

        @pl.when(jnp.logical_not(plain(q)))
        def _():
            ii_copy(q).wait()
            pend[slot] += irecv[1, 0:128, at_c].astype(jnp.float32)

        at_d = aligned(x * width + (q % steps) * CHUNK, CHUNK, CHUNK)

        @pl.when(flow == 0)
        def _():
            grad[:, at_d] = pend[slot, rows_mine]

        @pl.when(flow == 1)
        def _():
            pend[slot] += raw[:, at_c].astype(jnp.float32)
            fwd_out[:, at_d] = pend[slot, rows_mine].astype(jnp.bfloat16)

        dense[flow, 128:192, at_c] = pend[slot, rows_peer].astype(jnp.bfloat16)
        xb_copy(q).start()

    def finish(q):
        flow, at_c = place(q)
        at_d = aligned((1 - x) * width + (q % steps) * CHUNK, CHUNK, CHUNK)
        xb_copy(q).wait()

        @pl.when(flow == 0)
        def _():
            grad[:, at_d] = xrecv[0, :, at_c].astype(jnp.float32)

        @pl.when(flow == 1)
        def _():
            fwd_out[:, at_d] = xrecv[1, :, at_c]

    def each(first, last, stage):
        def one(q, carry):
            stage(q)
            return carry

        lax.fori_loop(first, last, one, 0)

    lax.fori_loop(0, steps, out_grad, 0)
    for h in range(2):
        for k in range(2):
            psend[1 + k, classes[h]] = acc[k, 1, classes[h]].astype(jnp.bfloat16)
            p_copy(1 + k, h).start()
    each(0, 2, add_pair)

    def gated(h):
        for k in range(2):
            p_copy(1 + k, h).wait()

        def some(i, carry):
            start_row = (1 - cls if h == 0 else cls) * 320
            at_i = aligned(start_row + i * 160, 160, 160)
            gate = acc[0, 0, at_i] + precv[1, at_i].astype(jnp.float32)
            upper = acc[1, 0, at_i] + precv[2, at_i].astype(jnp.float32)
            hid[0, at_i] = (gate * jax.nn.sigmoid(gate) * upper).astype(jnp.bfloat16)
            return carry

        lax.fori_loop(0, 2, some, 0)
        hid_copy(h).start()

    gated(0)
    each(2, 4, add_pair)
    gated(1)
    gres_copy.start()
    each(4, 5, add_pair)
    hid_copy(0).wait()

    def step(t, carry):
        @pl.when(t < steps)
        def _():
            out_rows(t)

        def stage(q, least, do):
            @pl.when((q >= least) & (q < 2 * steps))
            def _():
                do(q)

        def two_ways(q, least, do, do_odd):
            @pl.when((q >= least) & (q < 2 * steps) & plain(q))
            def _():
                do(q)

            @pl.when((q >= steps) & (q < 2 * steps) & jnp.logical_not(plain(q)))
            def _():
                do_odd(q)

        two_ways(t + 5, 5, add_pair, combine_all)

        @pl.when(t == 0)
        def _():
            each(0, 3, combine)
            add_outer(0)

        two_ways(t + 3, 3, combine, add_outer_all)
        stage(t + 1, 1, add_outer)
        stage(t - 1, 0, finish)

        @pl.when(t == steps + 1)
        def _():
            wait(u_loads)
            gres_copy.wait()
            bwd_out[:, cols_peer] = gres[...]

            def norm_back(i, carry):
                at_i = aligned(i * 16, 16, 16)
                at_u = [aligned(128 + k * 64 + i * 16, 16, 16) for k in range(2)]
                u = jnp.concatenate([packed[0, at_k] for at_k in at_u], axis=1).astype(jnp.float32)
                r = lax.rsqrt(jnp.mean(u * u, axis=1, keepdims=True) + EPSILON)
                h = grad[at_i] * gains[...]
                along = jnp.mean(h * u, axis=1, keepdims=True)
                result = r * h - u * (r * r * r * along)
                bwd_out[at_i] = (bwd_out[at_i].astype(jnp.float32) + result).astype(jnp.bfloat16)
                return carry

            lax.fori_loop(0, 4, norm_back, 0)

        return carry

    lax.fori_loop(0, 2 * steps + 1, step, 0)


def on_device(
    fwd_in, gains, gate_weight, up_weight, down_weight, fwd_routes, fwd_probs,
    bwd_grad, bwd_input, bwd_routes, bwd_probs, bwd_stash,
):
    depth = fwd_in.shape[2]
    width = depth // 2
    hidden = gate_weight.shape[2]
    r = np.arange(384)
    goal = np.where(r < 320, (r // 80) * 2 * CAP + r % CAP + 1000 * ((r % 80) // CAP), -1000000)
    goal = jnp.asarray(goal.reshape(1, 384), jnp.float32)
    bf, f32 = jnp.bfloat16, jnp.float32
    vmem, hbm = pl.BlockSpec(memory_space=pltpu.VMEM), pl.BlockSpec(memory_space=pl.ANY)
    dma = pltpu.SemaphoreType.DMA
    steps = width // CHUNK
    two = 2 * steps
    scratch = [
        pltpu.VMEM((64, 128), f32),
        pltpu.VMEM((512, 128), f32),
        pltpu.VMEM((24, 128), f32),
        pltpu.VMEM((128, 128), f32),
        pltpu.VMEM((128, width), bf),
        pltpu.VMEM((2, 256, width), bf),
        pltpu.VMEM((2, 320, width), bf),
        pltpu.VMEM((2, 640, width), bf),
        pltpu.VMEM((2, width, hidden), bf),
        pltpu.VMEM((2, width, hidden), bf),
        pltpu.VMEM((hidden, width), bf),
        pltpu.VMEM((hidden, width), bf),
        pltpu.VMEM((640, 2 * hidden), bf),
        pltpu.VMEM((2, 2, 640, hidden), f32),
        pltpu.VMEM((3, 640, hidden), bf),
        pltpu.VMEM((3, 640, hidden), bf),
        pltpu.VMEM((2, 2, 640, hidden), bf),
        pltpu.VMEM((2, 640, hidden), bf),
        pltpu.VMEM((2, 320, width), bf),
        pltpu.VMEM((steps, 320, CHUNK), f32),
        pltpu.VMEM((2, 320, width), bf),
        pltpu.VMEM((320, steps // 2 * CHUNK), bf),
        pltpu.VMEM((RING, 128, CHUNK), f32),
        pltpu.VMEM((2, 2, 128, CHUNK), f32),
        pltpu.VMEM((2, 128, width), bf),
        pltpu.VMEM((256, steps // 2 * CHUNK), bf),
        pltpu.VMEM((2, 64, width), bf),
        pltpu.VMEM((64, depth), f32),
        pltpu.VMEM((64, width), bf),
        pltpu.VMEM((2, 384, 256), bf),
        pltpu.VMEM((3, 2, 256, 384), bf),
        dma((2, PARTS, 2)), dma((2, PARTS, 2)),
        dma, dma,
        dma((2,)), dma((2,)),
        dma((7,)), dma((7,)),
        dma((2, PARTS)), dma((2, PARTS)),
        dma((2, PARTS, 3)), dma((2, PARTS, 3)),
        dma((2, PARTS)), dma((2, PARTS)),
        dma((2, steps)), dma((2, steps)),
        dma, dma,
        dma((3, 2)), dma((3, 2)),
        dma((2,)), dma((2,)),
        dma((2,)), dma((2,)),
        dma((two,)), dma((two,)),
        dma((steps // 2, 2, 3)), dma((steps // 2, 2, 3)), dma((steps // 2, 2)),
        dma((two, 3)), dma((two, 3)),
        dma((two,)), dma((two,)),
        dma((two,)), dma((two,)),
        dma((7,)), dma((2, PARTS)), dma((two,)),
    ]
    fwd_result, bwd_result = pl.pallas_call(
        kernel,
        out_shape=(jax.ShapeDtypeStruct((64, depth), bf), jax.ShapeDtypeStruct((64, depth), bf)),
        in_specs=[vmem, hbm, vmem, hbm, hbm, hbm, vmem, vmem, vmem, vmem, hbm, hbm, vmem],
        out_specs=(vmem, vmem),
        scratch_shapes=scratch,
        compiler_params=pltpu.CompilerParams(
            collective_id=0, has_side_effects=True, vmem_limit_bytes=63 * 1024 * 1024
        ),
        name="routed_experts",
    )(
        fwd_in[0], bwd_grad[0], gains, gate_weight[0], up_weight[0], down_weight[0],
        fwd_routes[0].T, fwd_probs[0].T, bwd_routes[0].T, bwd_probs[0].T, bwd_input[0], bwd_stash[0], goal,
    )
    return (fwd_result[None], bwd_result[None])


def solution(mesh):
    rows = P("section", "expert", None)
    cols = P("section", None, "expert")
    return jax.shard_map(
        on_device,
        mesh=mesh,
        in_specs=(rows, P("section", None), cols, cols, rows, rows, rows, rows, rows, rows, rows, rows),
        out_specs=(rows, rows),
        check_vma=False,
    )
```

```python
import jax
import jax.numpy as jnp
import numpy as np
from jax import lax
from jax.experimental import pallas as pl
from jax.experimental.pallas import tpu as pltpu
from jax.sharding import PartitionSpec as P

EPSILON = 1e-06
MESH = pl.DeviceIdType.MESH
CAP = 20
EARLY = 5

CHUNK = 512
LAG = 2
RING = LAG + 1
PARTS = 4
PIECE = 896
NT = (((1,), (1,)), ((), ()))


def mm(a, b):
    return jnp.dot(a, b, preferred_element_type=jnp.float32)


def mm_t(a, b):
    return lax.dot_general(a, b, NT, preferred_element_type=jnp.float32)


def aligned(start, size, unit):
    return pl.ds(pl.multiple_of(start, unit), size)


def slot_keys(first, second, offset):
    tokens = first.shape[1]
    expert = lax.broadcasted_iota(jnp.int32, (8, tokens), 0).astype(jnp.float32)
    one0 = jnp.where(first == expert, 1.0, 0.0)
    one1 = jnp.where(second == expert, 1.0, 0.0)
    row = lax.broadcasted_iota(jnp.int32, (tokens, tokens), 0)
    col = lax.broadcasted_iota(jnp.int32, (tokens, tokens), 1)
    earlier = jnp.where(row < col, 1.0, 0.0).astype(jnp.bfloat16)
    before = mm((one0 + one1).astype(jnp.bfloat16), earlier)
    pos0 = jnp.sum(one0 * before, axis=0, keepdims=True)
    pos1 = jnp.sum(one1 * before, axis=0, keepdims=True)
    return first * CAP + pos0 + offset, second * CAP + pos1 + offset


def kernel(
    fwd_in, bwd_grad, gains, wg, wu, wd, f_routes, f_probs, b_routes, b_probs, bwd_input, stash, target,
    outs,
    told, meta, scales, scale, raw, dense, packed, rows, w_own, w_peer, wd_own, wd_peer, st, acc, psend, precv, small, hid,
    irecv, ipend, back, back2, pend, pend2, orecv, orecv2, xrecv, grad, gres, pack, comb,
    relay_s, relay_r, gres_s, gres_r, scale_s, scale_r, meta_s, meta_r, o_s, o_r, z_s, z_r, i_s, i_r,
    wt_s, wt_r, wd_s, wd_r, p_s, p_r, sm_s, sm_r, hid_s, hid_r,
    ib_s, ib_r, zz_s, zz_r, zzloc, zb_s, zb_r, ob_s, ob_r, xb_s, xb_r, loc, zloc, zbloc,
):
    fwd_out, bwd_out = outs.at[0], outs.at[1]
    depth = gains.shape[1]
    width = depth // 2
    steps = width // CHUNK
    part = width // PARTS
    hidden = wg.shape[1]
    sec = lax.axis_index("section")
    ex = lax.axis_index("expert")
    z, y, x = ex // 8, (ex // 2) % 4, ex % 2
    half = y // 2
    cls = ((y + 1) // 2) % 2
    own = aligned(half * 128, 128, 128)
    other = aligned((1 - half) * 128, 128, 128)
    mine = aligned(half * 128 + x * 64, 64, 64)
    class_own = aligned(cls * 320, 320, 320)
    class_peer = aligned((1 - cls) * 320, 320, 320)
    cols_own = aligned(x * width, width, width)
    cols_peer = aligned((1 - x) * width, width, width)
    up, down = (sec + 1) % 4, (sec + 3) % 4

    def at(zz, yy, xx):
        return zz * 8 + yy * 2 + xx

    x_peer = (sec, at(z, y, 1 - x))
    o_peer = (sec, at(z, 3 - y, x))
    d_peer = (sec, at(z, 3 - y, 1 - x))
    i_peer = (sec, at(z, y + 1 - 2 * (y % 2), x))
    c_peers = [(sec, at(z, yy, xx)) for yy in (y + 1 - 2 * (y % 2), 2 + y % 2 - 2 * half) for xx in (x, 1 - x)]
    z_peers = [(sec, at((z + d) % 4, y, x)) for d in (1, 2, 3)]
    relays = [(s, at(z, y, xx)) for s in (up, down) for xx in (x, 1 - x)]

    barrier = pltpu.get_barrier_semaphore()
    partners = [x_peer, o_peer, d_peer] + c_peers + z_peers + relays
    for peer in partners:
        pl.semaphore_signal(barrier, inc=1, device_id=peer, device_id_type=MESH)
    pl.semaphore_wait(barrier, len(partners))

    def remote(src, dst, send, recv, peer):
        return pltpu.make_async_remote_copy(
            src_ref=src, dst_ref=dst, send_sem=send, recv_sem=recv, device_id=peer, device_id_type=MESH
        )

    def start(copies):
        for copy in copies:
            copy.start()

    def wait(copies):
        for copy in copies:
            copy.wait()

    def cols(k):
        return pl.ds(k * part, part)

    def relay(flow, k):
        src = (bwd_grad, fwd_in)[flow]
        copies = []
        for d, xx in enumerate((x, 1 - x)):
            dst = dense.at[0, mine, cols(k)] if flow == 0 else raw.at[aligned(x * 64, 64, 64), cols(k)]
            copies.append(remote(
                src.at[:, aligned(xx * width + k * part, part, 128)], dst,
                relay_s.at[flow, k, d], relay_r.at[flow, k, d], ((down, up)[flow], at(z, y, xx)),
            ))
        return copies

    def o_copy(flow, k):
        block = dense.at[flow, own, cols(k)]
        return remote(block, block, o_s.at[flow, k], o_r.at[flow, k], o_peer)

    def z_copies(flow, k):
        return [
            remote(
                packed.at[flow, aligned(((z + d) % 4) * 80, 80, 80), cols(k)],
                rows.at[flow, aligned(cls * 320 + z * 80, 80, 80), cols(k)],
                z_s.at[flow, k, d - 1], z_r.at[flow, k, d - 1], z_peers[d - 1],
            )
            for d in (1, 2, 3)
        ]

    def z_local(flow, k):
        return pltpu.make_async_copy(
            packed.at[flow, aligned(z * 80, 80, 80), cols(k)],
            rows.at[flow, aligned(cls * 320 + z * 80, 80, 80), cols(k)], zloc.at[flow, k],
        )

    def i_copy(flow, k):
        block = rows.at[flow, class_own, cols(k)]
        return remote(block, block, i_s.at[flow, k], i_r.at[flow, k], i_peer)

    gres_copy = remote(bwd_grad.at[:, cols_peer], gres, gres_s, gres_r, (down, at(z, y, x)))
    wd_copy = remote(wd.at[:, cols_peer], wd_peer, wd_s, wd_r, x_peer)

    def w_copies(c):
        return [
            remote(
                w.at[aligned((1 - x) * width + c * CHUNK, CHUNK, CHUNK)], w_peer.at[k, aligned(c * CHUNK, CHUNK, CHUNK)],
                wt_s.at[k, c], wt_r.at[k, c], x_peer,
            )
            for k, w in enumerate((wg, wu))
        ]

    for k in range(PARTS):
        start(relay(0, k))
    loads = [
        pltpu.make_async_copy(wd.at[:, cols_own], wd_own, loc.at[0]),
        pltpu.make_async_copy(stash.at[:, 0:hidden], small.at[0, 0], loc.at[1]),
        pltpu.make_async_copy(stash.at[:, hidden : 2 * hidden], small.at[1, 0], loc.at[4]),
        pltpu.make_async_copy(wg.at[cols_own], w_own.at[0], loc.at[2]),
        pltpu.make_async_copy(wu.at[cols_own], w_own.at[1], loc.at[3]),
    ]
    start(loads)

    offset = ((half * 2 + x) * 1000).astype(jnp.float32)
    lines = []
    for routes, probs in ((b_routes, b_probs), (f_routes, f_probs)):
        chosen = routes[...].astype(jnp.float32)
        lines += [*slot_keys(chosen[0:1], chosen[1:2], offset), probs[...]]
    lines = jnp.concatenate(lines, axis=0)
    my_lines = aligned((cls * 4 + half * 2 + x) * 8, 8, 8)
    told[my_lines] = jnp.concatenate([lines, jnp.zeros((8, 64), jnp.float32)], axis=1)
    meta_copies = [
        remote(told.at[my_lines], told.at[my_lines], meta_s.at[i], meta_r.at[i], peer)
        for i, peer in enumerate([x_peer, o_peer, d_peer] + c_peers)
    ]
    start(meta_copies)

    for i in range(4):
        v = fwd_in[pl.ds(i * 16, 16)].astype(jnp.float32)
        r = lax.rsqrt(jnp.mean(v * v, axis=1, keepdims=True) + EPSILON)
        scale[pl.ds(i * 16, 16)] = jnp.broadcast_to(r, (16, 128))
    turned = jnp.transpose(jnp.concatenate([scale[0:64], jnp.zeros((64, 128), jnp.float32)], axis=0))
    scales[16:24] = turned[0:8]
    scale_copies = [
        remote(
            scales.at[16:24], scales.at[aligned(x * 8, 8, 8)], scale_s.at[d], scale_r.at[d], (up, at(z, y, xx))
        )
        for d, xx in enumerate((x, 1 - x))
    ]
    start(scale_copies)
    for k in range(PARTS):
        start(relay(1, k))
    wd_copy.start()

    def norm(k):
        def some(i, carry):
            at_i = aligned(i * 16, 16, 16)
            v = raw[at_i, cols(k)].astype(jnp.float32)
            g = gains[:, aligned(x * width + k * part, part, 128)]
            dense[1, aligned(half * 128 + i * 16, 16, 16), cols(k)] = (v * scale[at_i, 0:1] * g).astype(jnp.bfloat16)
            return carry

        lax.fori_loop(0, 8, some, 0)

    def pack_rows(flow, k):
        o_copy(flow, k).wait()
        for j in range(part // PIECE):
            at_j = pl.ds(k * part + j * PIECE, PIECE)
            packed[flow, :, at_j] = mm(pack[flow, 0:320], dense[flow, :, at_j]).astype(jnp.bfloat16)
        start(z_copies(flow, k))
        z_local(flow, k).start()

    def pass_on(flow, k):
        wait(z_copies(flow, k))
        z_local(flow, k).wait()
        i_copy(flow, k).start()

    def relayed(flow, k):
        wait(relay(flow, k))
        if flow == 1:
            norm(k)
        o_copy(flow, k).start()

    goal = target[...] + (half * CAP).astype(jnp.float32)

    def column(group, i):
        return meta[aligned(group * 256, 256, 256), i : i + 1]

    def matches(group, i):
        return jnp.where(column(group, i) == goal, 1.0, 0.0)

    def build_pack(flow):
        pack[flow] = jnp.transpose(matches(cls, flow * 4) + matches(cls, flow * 4 + 1)).astype(jnp.bfloat16)

    def build_comb(at_i, group, base):
        weight = matches(group, base) * column(group, base + 2) + matches(group, base + 1) * column(group, base + 3)
        high = weight.astype(jnp.bfloat16)
        comb[at_i, 0] = high
        comb[at_i, 1] = (weight - high.astype(jnp.float32)).astype(jnp.bfloat16)

    relayed(0, 0)
    relayed(0, 1)
    wait(meta_copies)
    turned = jnp.transpose(jnp.concatenate([told[...], jnp.zeros((64, 128), jnp.float32)], axis=0))
    for i in range(8):
        meta[i * 64 : i * 64 + 64, 0:8] = turned[0:64, i * 8 : i * 8 + 8]
    build_pack(0)
    relayed(0, 2)
    pack_rows(0, 0)
    relayed(0, 3)
    pack_rows(0, 1)
    wait(scale_copies)
    both = jnp.concatenate([scales[0:1, 0:64], scales[8:9, 0:64]], axis=1)
    scale[...] = jnp.transpose(jnp.broadcast_to(both, (128, 128)))
    relayed(1, 0)
    pass_on(0, 0)
    pack_rows(0, 2)
    relayed(1, 1)
    pass_on(0, 1)
    pack_rows(0, 3)
    relayed(1, 2)
    build_pack(1)
    pass_on(0, 2)
    relayed(1, 3)
    start(w_copies(0))
    pass_on(0, 3)
    pack_rows(1, 0)
    pack_rows(1, 1)
    start(w_copies(1))
    pack_rows(1, 2)
    pass_on(1, 0)
    pack_rows(1, 3)
    pass_on(1, 1)
    start(w_copies(2))
    pass_on(1, 2)
    pass_on(1, 3)
    bwd_out[:, cols_own] = dense[0, mine]
    build_comb(0, cls, 0)
    build_comb(1, cls, 4)
    build_comb(2, 1 - cls, 4)
    wait(loads)
    for c, pair in enumerate(((0, 3), (1, 2))):
        for zz in range(4):
            for k in range(2):
                blocks = [small[k, 0, zz * 160 + yy * 40 : zz * 160 + yy * 40 + 40].astype(jnp.float32) for yy in pair]
                at_block = pl.ds(c * 320 + zz * 80, 80)
                st[at_block, k * hidden : (k + 1) * hidden] = jnp.concatenate(blocks, axis=0).astype(jnp.bfloat16)
    u_loads = [
        pltpu.make_async_copy(
            bwd_input.at[:, pl.ds(k * width, width)], packed.at[0, pl.ds(128 + k * 64, 64)], loc.at[5 + k]
        )
        for k in range(2)
    ]
    start(u_loads)

    wd_copy.wait()
    acc[...] = jnp.zeros_like(acc)
    for k in range(PARTS):
        i_copy(0, k).wait()

        def hid_grad(j, carry):
            at_j = aligned(k * part + j * PIECE, PIECE, 128)
            block = rows[0, :, at_j]
            acc[0, 0] += mm_t(block, wd_own[:, at_j])
            acc[0, 1] += mm_t(block, wd_peer[:, at_j])
            return carry

        lax.fori_loop(0, part // PIECE, hid_grad, 0)

    classes = (class_peer, class_own)

    def p_copy(i, h):
        return remote(psend.at[i, classes[h]], precv.at[i, classes[h]], p_s.at[i, h], p_r.at[i, h], x_peer)

    psend[0] = acc[0, 1].astype(jnp.bfloat16)
    for h in range(2):
        p_copy(0, h).start()
    for h in range(2):
        p_copy(0, h).wait()

    def gates(i, carry):
        at_i = aligned(i * 160, 160, 160)
        a = st[at_i, 0:hidden].astype(jnp.float32)
        b = st[at_i, hidden : 2 * hidden].astype(jnp.float32)
        sig = jax.nn.sigmoid(a)
        g = acc[0, 0, at_i] + precv[0, at_i].astype(jnp.float32)
        small[0, 0, at_i] = (g * b * sig * (1.0 + a * (1.0 - sig))).astype(jnp.bfloat16)
        small[1, 0, at_i] = (g * a * sig).astype(jnp.bfloat16)
        return carry

    lax.fori_loop(0, 4, gates, 0)
    small_copies = [remote(small.at[k, 0], small.at[k, 1], sm_s.at[k], sm_r.at[k], x_peer) for k in range(2)]
    start(small_copies)
    start(w_copies(3))
    acc[...] = jnp.zeros_like(acc)
    wait(small_copies)

    def hid_copy(h):
        return remote(hid.at[0, classes[h]], hid.at[1, classes[h]], hid_s.at[h], hid_r.at[h], x_peer)


    def plain(q):
        return (q < steps) | ((q - steps) % 2 == 0)

    def place(q):
        return q // steps, aligned((q % steps) * CHUNK, CHUNK, CHUNK)

    def ib_copy(q):
        flow, at_c = place(q)
        return remote(rows.at[flow, class_peer, at_c], irecv.at[flow, :, at_c], ib_s.at[q], ib_r.at[q], i_peer)

    def zb_copies(q):
        flow, at_c = place(q)
        return [
            remote(
                rows.at[flow, aligned(cls * 320 + ((z + d) % 4) * 80, 80, 80), at_c],
                back.at[flow, aligned(z * 80, 80, 80), at_c],
                zb_s.at[q, d - 1], zb_r.at[q, d - 1], z_peers[d - 1],
            )
            for d in (1, 2, 3)
        ]

    def zb_local(q):
        flow, at_c = place(q)
        return pltpu.make_async_copy(
            rows.at[flow, aligned(cls * 320 + z * 80, 80, 80), at_c],
            back.at[flow, aligned(z * 80, 80, 80), at_c], zbloc.at[q],
        )

    def ob_copy(q):
        flow, at_c = place(q)
        return remote(dense.at[flow, pl.ds(0, 128), at_c], orecv.at[flow, :, at_c], ob_s.at[q], ob_r.at[q], o_peer)

    def xb_copy(q):
        flow, at_c = place(q)
        return remote(dense.at[flow, pl.ds(128, 64), at_c], xrecv.at[flow, :, at_c], xb_s.at[q], xb_r.at[q], x_peer)

    def gate_sums(c):
        at_c = aligned(c * CHUNK, CHUNK, CHUNK)
        block = rows[1, :, at_c]
        for k in range(2):
            acc[k, 0] += mm(block, w_own[k, at_c])
            acc[k, 1] += mm(block, w_peer[k, at_c])

    def send_sums():
        for h in range(2):
            for k in range(2):
                psend[1 + k, classes[h]] = acc[k, 1, classes[h]].astype(jnp.bfloat16)
                p_copy(1 + k, h).start()

    def out_grad(c, carry):
        wait(w_copies(c))

        @pl.when(c + 4 < steps)
        def _():
            start(w_copies(c + 4))

        def out_chunk(q, carry):
            at_c = aligned(q * CHUNK, CHUNK, CHUNK)

            def total(at_rows):
                value = mm_t(small[0, 0, at_rows], w_own[0, at_c]) + mm_t(small[1, 0, at_rows], w_own[1, at_c])
                value += mm_t(small[0, 1, at_rows], w_peer[0, at_c])
                value += mm_t(small[1, 1, at_rows], w_peer[1, at_c])
                return value

            rows[0, class_peer, at_c] = total(class_peer).astype(jnp.bfloat16)
            ib_copy(q).start()
            ipend[q] = total(class_own)
            return carry

        @pl.when(c <= EARLY)
        def _():
            out_chunk(c, 0)

        @pl.when(c == EARLY)
        def _():
            for k in range(PARTS):
                i_copy(1, k).wait()

            def earlier(j, carry):
                gate_sums(j)
                return carry

            lax.fori_loop(0, EARLY, earlier, 0)

        @pl.when(c >= EARLY)
        def _():
            gate_sums(c)

        @pl.when(c == steps - 1)
        def _():
            send_sums()

        @pl.when(c > EARLY)
        def _():
            out_chunk(c, 0)

        return carry

    def out_rows(c):
        at_c = aligned(c * CHUNK, CHUNK, CHUNK)

        def total(at_rows):
            return mm(hid[0, at_rows], wd_own[:, at_c]) + mm(hid[1, at_rows], wd_peer[:, at_c])

        rows[1, class_peer, at_c] = total(class_peer).astype(jnp.bfloat16)

        @pl.when(c % 2 == 0)
        def _():
            ib_copy(steps + c).start()

        @pl.when(c % 2 == 1)
        def _():
            for j in range(3):
                zz_copy(c // 2, 0, j).start()
            zz_local(c // 2, 0).start()

        @pl.when(c == 0)
        def _():
            hid_copy(1).wait()

        @pl.when(c % 2 == 0)
        def _():
            ipend[c] = total(class_own)

        @pl.when(c % 2 == 1)
        def _():
            rows[1, class_own, at_c] = total(class_own).astype(jnp.bfloat16)
            for j in range(3):
                zz_copy(c // 2, 1, j).start()
            zz_local(c // 2, 1).start()

    def zz_copy(b, h, j):
        at_c = aligned((2 * b + 1) * CHUNK, CHUNK, CHUNK)
        src_row = ((1 - cls) if h == 0 else cls) * 320 + ((z + j + 1) % 4) * 80
        at_z = aligned(z * 80, 80, 80)
        dst = back2.at[at_z, aligned(b * CHUNK, CHUNK, CHUNK)] if h == 0 else back.at[1, at_z, at_c]
        return remote(
            rows.at[1, aligned(src_row, 80, 80), at_c], dst, zz_s.at[b, h, j], zz_r.at[b, h, j], z_peers[j]
        )

    def zz_local(b, h):
        at_c = aligned((2 * b + 1) * CHUNK, CHUNK, CHUNK)
        src_row = ((1 - cls) if h == 0 else cls) * 320 + z * 80
        at_z = aligned(z * 80, 80, 80)
        dst = back2.at[at_z, aligned(b * CHUNK, CHUNK, CHUNK)] if h == 0 else back.at[1, at_z, at_c]
        return pltpu.make_async_copy(rows.at[1, aligned(src_row, 80, 80), at_c], dst, zzloc.at[b, h])

    def oo_copy(q):
        _, at_c = place(q)
        b = (q - steps) // 2
        return remote(
            packed.at[1, pl.ds(0, 256), at_c], orecv2.at[:, aligned(b * CHUNK, CHUNK, CHUNK)],
            ob_s.at[q], ob_r.at[q], o_peer,
        )

    def ii_copy(q):
        _, at_c = place(q)
        return remote(packed.at[0, pl.ds(0, 128), at_c], irecv.at[1, pl.ds(0, 128), at_c], ib_s.at[q], ib_r.at[q], i_peer)

    def combine_all(q):
        _, at_c = place(q)
        b = (q - steps) // 2
        for h in range(2):
            for j in range(3):
                zz_copy(b, h, j).wait()
            zz_local(b, h).wait()
            i = 2 - h
            block = back2[:, aligned(b * CHUNK, CHUNK, CHUNK)] if h == 0 else back[1, :, at_c]
            away = mm(comb[i, 0, other, 0:320], block) + mm(comb[i, 1, other, 0:320], block)
            at_group = aligned(((1 - cls) if h == 0 else cls) * 128, 128, 128)
            packed[1, at_group, at_c] = away.astype(jnp.bfloat16)
            pend2[b % 2, h] = mm(comb[i, 0, own, 0:320], block) + mm(comb[i, 1, own, 0:320], block)
        oo_copy(q).start()

    def add_outer_all(q):
        _, at_c = place(q)
        b = (q - steps) // 2
        at_b = aligned(b * CHUNK, CHUNK, CHUNK)
        oo_copy(q).wait()
        peers = pend2[b % 2, 0] + orecv2[aligned((1 - cls) * 128, 128, 128), at_b].astype(jnp.float32)
        packed[0, 0:128, at_c] = peers.astype(jnp.bfloat16)
        ii_copy(q).start()
        pend[q % RING] = pend2[b % 2, 1] + orecv2[aligned(cls * 128, 128, 128), at_b].astype(jnp.float32)

    def add_pair(q):
        flow, at_c = place(q)
        ib_copy(q).wait()
        total = ipend[q % steps] + irecv[flow, :, at_c].astype(jnp.float32)
        rows[flow, class_own, at_c] = total.astype(jnp.bfloat16)
        start(zb_copies(q))
        zb_local(q).start()

    def combine(q):
        flow, at_c = place(q)
        wait(zb_copies(q))
        zb_local(q).wait()
        block = back[flow, :, at_c]
        away = mm(comb[flow, 0, other, 0:320], block) + mm(comb[flow, 1, other, 0:320], block)
        dense[flow, 0:128, at_c] = away.astype(jnp.bfloat16)
        ob_copy(q).start()
        pend[q % RING] = mm(comb[flow, 0, own, 0:320], block) + mm(comb[flow, 1, own, 0:320], block)

    def add_outer(q):
        flow, at_c = place(q)
        slot = q % RING
        rows_mine, rows_peer = aligned(x * 64, 64, 64), aligned((1 - x) * 64, 64, 64)

        @pl.when(plain(q))
        def _():
            ob_copy(q).wait()
            pend[slot] += orecv[flow, :, at_c].astype(jnp.float32)

        @pl.when(jnp.logical_not(plain(q)))
        def _():
            ii_copy(q).wait()
            pend[slot] += irecv[1, 0:128, at_c].astype(jnp.float32)

        at_d = aligned(x * width + (q % steps) * CHUNK, CHUNK, CHUNK)

        @pl.when(flow == 0)
        def _():
            grad[:, at_d] = pend[slot, rows_mine]

        @pl.when(flow == 1)
        def _():
            pend[slot] += raw[:, at_c].astype(jnp.float32)
            fwd_out[:, at_d] = pend[slot, rows_mine].astype(jnp.bfloat16)

        dense[flow, 128:192, at_c] = pend[slot, rows_peer].astype(jnp.bfloat16)
        xb_copy(q).start()

    def finish(q):
        flow, at_c = place(q)
        at_d = aligned((1 - x) * width + (q % steps) * CHUNK, CHUNK, CHUNK)
        xb_copy(q).wait()

        @pl.when(flow == 0)
        def _():
            grad[:, at_d] = xrecv[0, :, at_c].astype(jnp.float32)

        @pl.when(flow == 1)
        def _():
            fwd_out[:, at_d] = xrecv[1, :, at_c]

    def each(first, last, stage):
        def one(q, carry):
            stage(q)
            return carry

        lax.fori_loop(first, last, one, 0)

    lax.fori_loop(0, steps, out_grad, 0)
    each(0, 4, add_pair)
    each(0, 3, combine)
    add_outer(0)

    def gated(h):
        for k in range(2):
            p_copy(1 + k, h).wait()

        def some(i, carry):
            start_row = (1 - cls if h == 0 else cls) * 320
            at_i = aligned(start_row + i * 160, 160, 160)
            gate = acc[0, 0, at_i] + precv[1, at_i].astype(jnp.float32)
            upper = acc[1, 0, at_i] + precv[2, at_i].astype(jnp.float32)
            hid[0, at_i] = (gate * jax.nn.sigmoid(gate) * upper).astype(jnp.bfloat16)
            return carry

        lax.fori_loop(0, 2, some, 0)
        hid_copy(h).start()

    gated(0)
    add_pair(4)
    combine(3)
    add_outer(1)
    gated(1)
    gres_copy.start()
    add_pair(5)
    combine(4)
    add_outer(2)
    hid_copy(0).wait()

    def step(t, carry):
        @pl.when(t < steps)
        def _():
            out_rows(t)

        def stage(q, least, do):
            @pl.when((q >= least) & (q < 2 * steps))
            def _():
                do(q)

        def two_ways(q, least, do, do_odd):
            @pl.when((q >= least) & (q < 2 * steps) & plain(q))
            def _():
                do(q)

            @pl.when((q >= steps) & (q < 2 * steps) & jnp.logical_not(plain(q)))
            def _():
                do_odd(q)

        two_ways(t + steps - LAG, 6, add_pair, combine_all)

        two_ways(t + steps - 2 * LAG, 5, combine, add_outer_all)
        stage(t + steps - 3 * LAG, 3, add_outer)
        stage(t + steps - 4 * LAG, max(0, steps - 4 * LAG), finish)

        @pl.when(t == 4 * LAG - 1)
        def _():
            wait(u_loads)
            gres_copy.wait()
            bwd_out[:, cols_peer] = gres[...]

            def norm_back(i, carry):
                at_i = aligned(i * 16, 16, 16)
                at_u = [aligned(128 + k * 64 + i * 16, 16, 16) for k in range(2)]
                u = jnp.concatenate([packed[0, at_k] for at_k in at_u], axis=1).astype(jnp.float32)
                r = lax.rsqrt(jnp.mean(u * u, axis=1, keepdims=True) + EPSILON)
                h = grad[at_i] * gains[...]
                along = jnp.mean(h * u, axis=1, keepdims=True)
                result = r * h - u * (r * r * r * along)
                bwd_out[at_i] = (bwd_out[at_i].astype(jnp.float32) + result).astype(jnp.bfloat16)
                return carry

            lax.fori_loop(0, 4, norm_back, 0)

        return carry

    lax.fori_loop(0, steps + 4 * LAG, step, 0)


def on_device(
    fwd_in, gains, gate_weight, up_weight, down_weight, fwd_routes, fwd_probs,
    bwd_grad, bwd_input, bwd_routes, bwd_probs, bwd_stash,
):
    depth = fwd_in.shape[2]
    width = depth // 2
    hidden = gate_weight.shape[2]
    r = np.arange(384)
    goal = np.where(r < 320, (r // 80) * 2 * CAP + r % CAP + 1000 * ((r % 80) // CAP), -1000000)
    goal = jnp.asarray(goal.reshape(1, 384), jnp.float32)
    bf, f32 = jnp.bfloat16, jnp.float32
    vmem, hbm = pl.BlockSpec(memory_space=pltpu.VMEM), pl.BlockSpec(memory_space=pl.ANY)
    dma = pltpu.SemaphoreType.DMA
    steps = width // CHUNK
    two = 2 * steps
    scratch = [
        pltpu.VMEM((64, 128), f32),
        pltpu.VMEM((512, 128), f32),
        pltpu.VMEM((24, 128), f32),
        pltpu.VMEM((128, 128), f32),
        pltpu.VMEM((128, width), bf),
        pltpu.VMEM((2, 256, width), bf),
        pltpu.VMEM((2, 320, width), bf),
        pltpu.VMEM((2, 640, width), bf),
        pltpu.VMEM((2, width, hidden), bf),
        pltpu.VMEM((2, width, hidden), bf),
        pltpu.VMEM((hidden, width), bf),
        pltpu.VMEM((hidden, width), bf),
        pltpu.VMEM((640, 2 * hidden), bf),
        pltpu.VMEM((2, 2, 640, hidden), f32),
        pltpu.VMEM((3, 640, hidden), bf),
        pltpu.VMEM((3, 640, hidden), bf),
        pltpu.VMEM((2, 2, 640, hidden), bf),
        pltpu.VMEM((2, 640, hidden), bf),
        pltpu.VMEM((2, 320, width), bf),
        pltpu.VMEM((steps, 320, CHUNK), f32),
        pltpu.VMEM((2, 320, width), bf),
        pltpu.VMEM((320, steps // 2 * CHUNK), bf),
        pltpu.VMEM((RING, 128, CHUNK), f32),
        pltpu.VMEM((2, 2, 128, CHUNK), f32),
        pltpu.VMEM((2, 128, width), bf),
        pltpu.VMEM((256, steps // 2 * CHUNK), bf),
        pltpu.VMEM((2, 64, width), bf),
        pltpu.VMEM((64, depth), f32),
        pltpu.VMEM((64, width), bf),
        pltpu.VMEM((2, 384, 256), bf),
        pltpu.VMEM((3, 2, 256, 384), bf),
        dma((2, PARTS, 2)), dma((2, PARTS, 2)),
        dma, dma,
        dma((2,)), dma((2,)),
        dma((7,)), dma((7,)),
        dma((2, PARTS)), dma((2, PARTS)),
        dma((2, PARTS, 3)), dma((2, PARTS, 3)),
        dma((2, PARTS)), dma((2, PARTS)),
        dma((2, width // CHUNK)), dma((2, width // CHUNK)),
        dma, dma,
        dma((3, 2)), dma((3, 2)),
        dma((2,)), dma((2,)),
        dma((2,)), dma((2,)),
        dma((two,)), dma((two,)),
        dma((steps // 2, 2, 3)), dma((steps // 2, 2, 3)), dma((steps // 2, 2)),
        dma((two, 3)), dma((two, 3)),
        dma((two,)), dma((two,)),
        dma((two,)), dma((two,)),
        dma((7,)), dma((2, PARTS)), dma((two,)),
    ]
    outs = pl.pallas_call(
        kernel,
        out_shape=jax.ShapeDtypeStruct((2, 64, depth), bf),
        in_specs=[vmem, hbm, vmem, hbm, hbm, hbm, vmem, vmem, vmem, vmem, hbm, hbm, vmem],
        out_specs=vmem,
        scratch_shapes=scratch,
        compiler_params=pltpu.CompilerParams(
            collective_id=0, has_side_effects=True, vmem_limit_bytes=63 * 1024 * 1024
        ),
        name="routed_experts",
    )(
        fwd_in[0], bwd_grad[0], gains, gate_weight[0], up_weight[0], down_weight[0],
        fwd_routes[0].T, fwd_probs[0].T, bwd_routes[0].T, bwd_probs[0].T, bwd_input[0], bwd_stash[0], goal,
    )
    return (outs[0:1], outs[1:2])


def solution(mesh):
    rows = P("section", "expert", None)
    cols = P("section", None, "expert")
    return jax.shard_map(
        on_device,
        mesh=mesh,
        in_specs=(rows, P("section", None), cols, cols, rows, rows, rows, rows, rows, rows, rows, rows),
        out_specs=(rows, rows),
        check_vma=False,
    )
```

```python
import jax
import jax.numpy as jnp
import numpy as np
from jax import lax
from jax.experimental import pallas as pl
from jax.experimental.pallas import tpu as pltpu
from jax.sharding import PartitionSpec as P

EPSILON = 1e-06
MESH = pl.DeviceIdType.MESH
CAP = 20
EARLY = 5

CHUNK = 512
LAG = 2
RING = LAG + 1
PARTS = 4
PIECE = 896
NT = (((1,), (1,)), ((), ()))


def mm(a, b):
    return jnp.dot(a, b, preferred_element_type=jnp.float32)


def mm_t(a, b):
    return lax.dot_general(a, b, NT, preferred_element_type=jnp.float32)


def aligned(start, size, unit):
    return pl.ds(pl.multiple_of(start, unit), size)


def slot_keys(first, second, offset):
    tokens = first.shape[1]
    expert = lax.broadcasted_iota(jnp.int32, (8, tokens), 0).astype(jnp.float32)
    one0 = jnp.where(first == expert, 1.0, 0.0)
    one1 = jnp.where(second == expert, 1.0, 0.0)
    row = lax.broadcasted_iota(jnp.int32, (tokens, tokens), 0)
    col = lax.broadcasted_iota(jnp.int32, (tokens, tokens), 1)
    earlier = jnp.where(row < col, 1.0, 0.0).astype(jnp.bfloat16)
    before = mm((one0 + one1).astype(jnp.bfloat16), earlier)
    pos0 = jnp.sum(one0 * before, axis=0, keepdims=True)
    pos1 = jnp.sum(one1 * before, axis=0, keepdims=True)
    return first * CAP + pos0 + offset, second * CAP + pos1 + offset


def kernel(
    fwd_in, bwd_grad, gains, wg, wu, wd, f_routes, f_probs, b_routes, b_probs, bwd_input, stash, target,
    outs,
    told, meta, scales, scale, raw, dense, packed, rows, w_own, w_peer, wd_own, wd_peer, st, acc, psend, precv, small, hid,
    irecv, ipend, back, back2, pend, pend2, orecv, orecv2, xrecv, grad, gres, pack, comb,
    relay_s, relay_r, gres_s, gres_r, scale_s, scale_r, meta_s, meta_r, o_s, o_r, z_s, z_r, i_s, i_r,
    wt_s, wt_r, wd_s, wd_r, p_s, p_r, sm_s, sm_r, hid_s, hid_r,
    ib_s, ib_r, zz_s, zz_r, zzloc, zb_s, zb_r, ob_s, ob_r, xb_s, xb_r, loc, zloc, zbloc,
):
    fwd_out, bwd_out = outs.at[0], outs.at[1]
    depth = gains.shape[1]
    width = depth // 2
    steps = width // CHUNK
    part = width // PARTS
    hidden = wg.shape[1]
    sec = lax.axis_index("section")
    ex = lax.axis_index("expert")
    z, y, x = ex // 8, (ex // 2) % 4, ex % 2
    half = y // 2
    cls = ((y + 1) // 2) % 2
    own = aligned(half * 128, 128, 128)
    other = aligned((1 - half) * 128, 128, 128)
    mine = aligned(half * 128 + x * 64, 64, 64)
    class_own = aligned(cls * 320, 320, 320)
    class_peer = aligned((1 - cls) * 320, 320, 320)
    cols_own = aligned(x * width, width, width)
    cols_peer = aligned((1 - x) * width, width, width)
    up, down = (sec + 1) % 4, (sec + 3) % 4

    def at(zz, yy, xx):
        return zz * 8 + yy * 2 + xx

    x_peer = (sec, at(z, y, 1 - x))
    o_peer = (sec, at(z, 3 - y, x))
    d_peer = (sec, at(z, 3 - y, 1 - x))
    i_peer = (sec, at(z, y + 1 - 2 * (y % 2), x))
    c_peers = [(sec, at(z, yy, xx)) for yy in (y + 1 - 2 * (y % 2), 2 + y % 2 - 2 * half) for xx in (x, 1 - x)]
    z_peers = [(sec, at((z + d) % 4, y, x)) for d in (1, 2, 3)]
    relays = [(s, at(z, y, xx)) for s in (up, down) for xx in (x, 1 - x)]

    barrier = pltpu.get_barrier_semaphore()
    partners = [x_peer, o_peer, d_peer] + c_peers + z_peers + relays
    for peer in partners:
        pl.semaphore_signal(barrier, inc=1, device_id=peer, device_id_type=MESH)
    pl.semaphore_wait(barrier, len(partners))

    def remote(src, dst, send, recv, peer):
        return pltpu.make_async_remote_copy(
            src_ref=src, dst_ref=dst, send_sem=send, recv_sem=recv, device_id=peer, device_id_type=MESH
        )

    def start(copies):
        for copy in copies:
            copy.start()

    def wait(copies):
        for copy in copies:
            copy.wait()

    def cols(k):
        return pl.ds(k * part, part)

    def relay(flow, k):
        src = (bwd_grad, fwd_in)[flow]
        copies = []
        for d, xx in enumerate((x, 1 - x)):
            dst = dense.at[0, mine, cols(k)] if flow == 0 else raw.at[aligned(x * 64, 64, 64), cols(k)]
            copies.append(remote(
                src.at[:, aligned(xx * width + k * part, part, 128)], dst,
                relay_s.at[flow, k, d], relay_r.at[flow, k, d], ((down, up)[flow], at(z, y, xx)),
            ))
        return copies

    def o_copy(flow, k):
        block = dense.at[flow, own, cols(k)]
        return remote(block, block, o_s.at[flow, k], o_r.at[flow, k], o_peer)

    def z_copies(flow, k):
        return [
            remote(
                packed.at[flow, aligned(((z + d) % 4) * 80, 80, 80), cols(k)],
                rows.at[flow, aligned(cls * 320 + z * 80, 80, 80), cols(k)],
                z_s.at[flow, k, d - 1], z_r.at[flow, k, d - 1], z_peers[d - 1],
            )
            for d in (1, 2, 3)
        ]

    def z_local(flow, k):
        return pltpu.make_async_copy(
            packed.at[flow, aligned(z * 80, 80, 80), cols(k)],
            rows.at[flow, aligned(cls * 320 + z * 80, 80, 80), cols(k)], zloc.at[flow, k],
        )

    def i_copy(flow, k):
        block = rows.at[flow, class_own, cols(k)]
        return remote(block, block, i_s.at[flow, k], i_r.at[flow, k], i_peer)

    gres_copy = remote(bwd_grad.at[:, cols_peer], gres, gres_s, gres_r, (down, at(z, y, x)))
    wd_copy = remote(wd.at[:, cols_peer], wd_peer, wd_s, wd_r, x_peer)

    def w_copies(c):
        return [
            remote(
                w.at[aligned((1 - x) * width + c * CHUNK, CHUNK, CHUNK)], w_peer.at[k, aligned(c * CHUNK, CHUNK, CHUNK)],
                wt_s.at[k, c], wt_r.at[k, c], x_peer,
            )
            for k, w in enumerate((wg, wu))
        ]

    for k in range(PARTS):
        start(relay(0, k))
    loads = [
        pltpu.make_async_copy(wd.at[:, cols_own], wd_own, loc.at[0]),
        pltpu.make_async_copy(stash.at[:, 0:hidden], small.at[0, 0], loc.at[1]),
        pltpu.make_async_copy(stash.at[:, hidden : 2 * hidden], small.at[1, 0], loc.at[4]),
        pltpu.make_async_copy(wg.at[cols_own], w_own.at[0], loc.at[2]),
        pltpu.make_async_copy(wu.at[cols_own], w_own.at[1], loc.at[3]),
    ]
    start(loads)

    offset = ((half * 2 + x) * 1000).astype(jnp.float32)
    lines = []
    for routes, probs in ((b_routes, b_probs), (f_routes, f_probs)):
        chosen = routes[...].astype(jnp.float32)
        lines += [*slot_keys(chosen[0:1], chosen[1:2], offset), probs[...]]
    lines = jnp.concatenate(lines, axis=0)
    my_lines = aligned((cls * 4 + half * 2 + x) * 8, 8, 8)
    told[my_lines] = jnp.concatenate([lines, jnp.zeros((8, 64), jnp.float32)], axis=1)
    meta_copies = [
        remote(told.at[my_lines], told.at[my_lines], meta_s.at[i], meta_r.at[i], peer)
        for i, peer in enumerate([x_peer, o_peer, d_peer] + c_peers)
    ]
    start(meta_copies)

    for i in range(4):
        v = fwd_in[pl.ds(i * 16, 16)].astype(jnp.float32)
        r = lax.rsqrt(jnp.mean(v * v, axis=1, keepdims=True) + EPSILON)
        scale[pl.ds(i * 16, 16)] = jnp.broadcast_to(r, (16, 128))
    turned = jnp.transpose(jnp.concatenate([scale[0:64], jnp.zeros((64, 128), jnp.float32)], axis=0))
    scales[16:24] = turned[0:8]
    scale_copies = [
        remote(
            scales.at[16:24], scales.at[aligned(x * 8, 8, 8)], scale_s.at[d], scale_r.at[d], (up, at(z, y, xx))
        )
        for d, xx in enumerate((x, 1 - x))
    ]
    start(scale_copies)
    for k in range(PARTS):
        start(relay(1, k))
    wd_copy.start()

    def norm(k):
        def some(i, carry):
            at_i = aligned(i * 16, 16, 16)
            v = raw[at_i, cols(k)].astype(jnp.float32)
            g = gains[:, aligned(x * width + k * part, part, 128)]
            dense[1, aligned(half * 128 + i * 16, 16, 16), cols(k)] = (v * scale[at_i, 0:1] * g).astype(jnp.bfloat16)
            return carry

        lax.fori_loop(0, 8, some, 0)

    def pack_rows(flow, k):
        o_copy(flow, k).wait()
        for j in range(part // PIECE):
            at_j = pl.ds(k * part + j * PIECE, PIECE)
            packed[flow, :, at_j] = mm(pack[flow, 0:320], dense[flow, :, at_j]).astype(jnp.bfloat16)
        start(z_copies(flow, k))
        z_local(flow, k).start()

    def pass_on(flow, k):
        wait(z_copies(flow, k))
        z_local(flow, k).wait()
        i_copy(flow, k).start()

    def relayed(flow, k):
        wait(relay(flow, k))
        if flow == 1:
            norm(k)
        o_copy(flow, k).start()

    goal = target[...] + (half * CAP).astype(jnp.float32)

    def column(group, i):
        return meta[aligned(group * 256, 256, 256), i : i + 1]

    def matches(group, i):
        return jnp.where(column(group, i) == goal, 1.0, 0.0)

    def build_pack(flow):
        pack[flow] = jnp.transpose(matches(cls, flow * 4) + matches(cls, flow * 4 + 1)).astype(jnp.bfloat16)

    def build_comb(at_i, group, base):
        weight = matches(group, base) * column(group, base + 2) + matches(group, base + 1) * column(group, base + 3)
        high = weight.astype(jnp.bfloat16)
        comb[at_i, 0] = high
        comb[at_i, 1] = (weight - high.astype(jnp.float32)).astype(jnp.bfloat16)

    relayed(0, 0)
    relayed(0, 1)
    wait(meta_copies)
    turned = jnp.transpose(jnp.concatenate([told[...], jnp.zeros((64, 128), jnp.float32)], axis=0))
    for i in range(8):
        meta[i * 64 : i * 64 + 64, 0:8] = turned[0:64, i * 8 : i * 8 + 8]
    build_pack(0)
    relayed(0, 2)
    pack_rows(0, 0)
    relayed(0, 3)
    pack_rows(0, 1)
    wait(scale_copies)
    both = jnp.concatenate([scales[0:1, 0:64], scales[8:9, 0:64]], axis=1)
    scale[...] = jnp.transpose(jnp.broadcast_to(both, (128, 128)))
    relayed(1, 0)
    pass_on(0, 0)
    pack_rows(0, 2)
    relayed(1, 1)
    pass_on(0, 1)
    pack_rows(0, 3)
    relayed(1, 2)
    build_pack(1)
    pass_on(0, 2)
    relayed(1, 3)
    start(w_copies(0))
    pass_on(0, 3)
    pack_rows(1, 0)
    pack_rows(1, 1)
    start(w_copies(1))
    pack_rows(1, 2)
    pass_on(1, 0)
    pack_rows(1, 3)
    pass_on(1, 1)
    start(w_copies(2))
    pass_on(1, 2)
    pass_on(1, 3)
    bwd_out[:, cols_own] = dense[0, mine]
    build_comb(0, cls, 0)
    build_comb(1, cls, 4)
    build_comb(2, 1 - cls, 4)
    wait(loads)
    for c, pair in enumerate(((0, 3), (1, 2))):
        for zz in range(4):
            for k in range(2):
                wide = small[k, 0, zz * 160 : zz * 160 + 160].astype(jnp.float32)
                blocks = [wide[yy * 40 : yy * 40 + 40] for yy in pair]
                at_block = pl.ds(c * 320 + zz * 80, 80)
                st[at_block, k * hidden : (k + 1) * hidden] = jnp.concatenate(blocks, axis=0).astype(jnp.bfloat16)
    u_loads = [
        pltpu.make_async_copy(
            bwd_input.at[:, pl.ds(k * width, width)], packed.at[0, pl.ds(128 + k * 64, 64)], loc.at[5 + k]
        )
        for k in range(2)
    ]
    start(u_loads)

    wd_copy.wait()
    acc[...] = jnp.zeros_like(acc)
    for k in range(PARTS):
        i_copy(0, k).wait()

        def hid_grad(j, carry):
            at_j = aligned(k * part + j * PIECE, PIECE, 128)
            block = rows[0, :, at_j]
            acc[0, 0] += mm_t(block, wd_own[:, at_j])
            acc[0, 1] += mm_t(block, wd_peer[:, at_j])
            return carry

        lax.fori_loop(0, part // PIECE, hid_grad, 0)

    classes = (class_peer, class_own)

    def p_copy(i, h):
        return remote(psend.at[i, classes[h]], precv.at[i, classes[h]], p_s.at[i, h], p_r.at[i, h], x_peer)

    psend[0] = acc[0, 1].astype(jnp.bfloat16)
    for h in range(2):
        p_copy(0, h).start()
    for h in range(2):
        p_copy(0, h).wait()

    def gates(i, carry):
        at_i = aligned(i * 160, 160, 160)
        a = st[at_i, 0:hidden].astype(jnp.float32)
        b = st[at_i, hidden : 2 * hidden].astype(jnp.float32)
        sig = jax.nn.sigmoid(a)
        g = acc[0, 0, at_i] + precv[0, at_i].astype(jnp.float32)
        small[0, 0, at_i] = (g * b * sig * (1.0 + a * (1.0 - sig))).astype(jnp.bfloat16)
        small[1, 0, at_i] = (g * a * sig).astype(jnp.bfloat16)
        return carry

    lax.fori_loop(0, 4, gates, 0)
    small_copies = [remote(small.at[k, 0], small.at[k, 1], sm_s.at[k], sm_r.at[k], x_peer) for k in range(2)]
    start(small_copies)
    start(w_copies(3))
    acc[...] = jnp.zeros_like(acc)
    wait(small_copies)

    def hid_copy(h):
        return remote(hid.at[0, classes[h]], hid.at[1, classes[h]], hid_s.at[h], hid_r.at[h], x_peer)


    def plain(q):
        return (q < steps) | ((q - steps) % 2 == 0)

    def place(q):
        return q // steps, aligned((q % steps) * CHUNK, CHUNK, CHUNK)

    def ib_copy(q):
        flow, at_c = place(q)
        return remote(rows.at[flow, class_peer, at_c], irecv.at[flow, :, at_c], ib_s.at[q], ib_r.at[q], i_peer)

    def zb_copies(q):
        flow, at_c = place(q)
        return [
            remote(
                rows.at[flow, aligned(cls * 320 + ((z + d) % 4) * 80, 80, 80), at_c],
                back.at[flow, aligned(z * 80, 80, 80), at_c],
                zb_s.at[q, d - 1], zb_r.at[q, d - 1], z_peers[d - 1],
            )
            for d in (1, 2, 3)
        ]

    def zb_local(q):
        flow, at_c = place(q)
        return pltpu.make_async_copy(
            rows.at[flow, aligned(cls * 320 + z * 80, 80, 80), at_c],
            back.at[flow, aligned(z * 80, 80, 80), at_c], zbloc.at[q],
        )

    def ob_copy(q):
        flow, at_c = place(q)
        return remote(dense.at[flow, pl.ds(0, 128), at_c], orecv.at[flow, :, at_c], ob_s.at[q], ob_r.at[q], o_peer)

    def xb_copy(q):
        flow, at_c = place(q)
        return remote(dense.at[flow, pl.ds(128, 64), at_c], xrecv.at[flow, :, at_c], xb_s.at[q], xb_r.at[q], x_peer)

    def gate_sums(c):
        at_c = aligned(c * CHUNK, CHUNK, CHUNK)
        block = rows[1, :, at_c]
        for k in range(2):
            acc[k, 0] += mm(block, w_own[k, at_c])
            acc[k, 1] += mm(block, w_peer[k, at_c])

    def send_sums():
        for h in range(2):
            for k in range(2):
                psend[1 + k, classes[h]] = acc[k, 1, classes[h]].astype(jnp.bfloat16)
                p_copy(1 + k, h).start()

    def out_grad(c, carry):
        wait(w_copies(c))

        @pl.when(c + 4 < steps)
        def _():
            start(w_copies(c + 4))

        def out_chunk(q, carry):
            at_c = aligned(q * CHUNK, CHUNK, CHUNK)

            def total(at_rows):
                value = mm_t(small[0, 0, at_rows], w_own[0, at_c]) + mm_t(small[1, 0, at_rows], w_own[1, at_c])
                value += mm_t(small[0, 1, at_rows], w_peer[0, at_c])
                value += mm_t(small[1, 1, at_rows], w_peer[1, at_c])
                return value

            rows[0, class_peer, at_c] = total(class_peer).astype(jnp.bfloat16)
            ib_copy(q).start()
            ipend[q] = total(class_own)
            return carry

        @pl.when(c <= EARLY)
        def _():
            out_chunk(c, 0)

        @pl.when(c == EARLY)
        def _():
            for k in range(PARTS):
                i_copy(1, k).wait()

            def earlier(j, carry):
                gate_sums(j)
                return carry

            lax.fori_loop(0, EARLY, earlier, 0)

        @pl.when(c >= EARLY)
        def _():
            gate_sums(c)

        @pl.when(c == steps - 1)
        def _():
            send_sums()

        @pl.when(c > EARLY)
        def _():
            out_chunk(c, 0)

        return carry

    def out_rows(c):
        at_c = aligned(c * CHUNK, CHUNK, CHUNK)

        def total(at_rows):
            return mm(hid[0, at_rows], wd_own[:, at_c]) + mm(hid[1, at_rows], wd_peer[:, at_c])

        rows[1, class_peer, at_c] = total(class_peer).astype(jnp.bfloat16)

        @pl.when(c % 2 == 0)
        def _():
            ib_copy(steps + c).start()

        @pl.when(c % 2 == 1)
        def _():
            for j in range(3):
                zz_copy(c // 2, 0, j).start()
            zz_local(c // 2, 0).start()

        @pl.when(c == 0)
        def _():
            hid_copy(1).wait()

        @pl.when(c % 2 == 0)
        def _():
            ipend[c] = total(class_own)

        @pl.when(c % 2 == 1)
        def _():
            rows[1, class_own, at_c] = total(class_own).astype(jnp.bfloat16)
            for j in range(3):
                zz_copy(c // 2, 1, j).start()
            zz_local(c // 2, 1).start()

    def zz_copy(b, h, j):
        at_c = aligned((2 * b + 1) * CHUNK, CHUNK, CHUNK)
        src_row = ((1 - cls) if h == 0 else cls) * 320 + ((z + j + 1) % 4) * 80
        at_z = aligned(z * 80, 80, 80)
        dst = back2.at[at_z, aligned(b * CHUNK, CHUNK, CHUNK)] if h == 0 else back.at[1, at_z, at_c]
        return remote(
            rows.at[1, aligned(src_row, 80, 80), at_c], dst, zz_s.at[b, h, j], zz_r.at[b, h, j], z_peers[j]
        )

    def zz_local(b, h):
        at_c = aligned((2 * b + 1) * CHUNK, CHUNK, CHUNK)
        src_row = ((1 - cls) if h == 0 else cls) * 320 + z * 80
        at_z = aligned(z * 80, 80, 80)
        dst = back2.at[at_z, aligned(b * CHUNK, CHUNK, CHUNK)] if h == 0 else back.at[1, at_z, at_c]
        return pltpu.make_async_copy(rows.at[1, aligned(src_row, 80, 80), at_c], dst, zzloc.at[b, h])

    def oo_copy(q):
        _, at_c = place(q)
        b = (q - steps) // 2
        return remote(
            packed.at[1, pl.ds(0, 256), at_c], orecv2.at[:, aligned(b * CHUNK, CHUNK, CHUNK)],
            ob_s.at[q], ob_r.at[q], o_peer,
        )

    def ii_copy(q):
        _, at_c = place(q)
        return remote(packed.at[0, pl.ds(0, 128), at_c], irecv.at[1, pl.ds(0, 128), at_c], ib_s.at[q], ib_r.at[q], i_peer)

    def combine_all(q):
        _, at_c = place(q)
        b = (q - steps) // 2
        for h in range(2):
            for j in range(3):
                zz_copy(b, h, j).wait()
            zz_local(b, h).wait()
            i = 2 - h
            block = back2[:, aligned(b * CHUNK, CHUNK, CHUNK)] if h == 0 else back[1, :, at_c]
            away = mm(comb[i, 0, other, 0:320], block) + mm(comb[i, 1, other, 0:320], block)
            at_group = aligned(((1 - cls) if h == 0 else cls) * 128, 128, 128)
            packed[1, at_group, at_c] = away.astype(jnp.bfloat16)
            pend2[b % 2, h] = mm(comb[i, 0, own, 0:320], block) + mm(comb[i, 1, own, 0:320], block)
        oo_copy(q).start()

    def add_outer_all(q):
        _, at_c = place(q)
        b = (q - steps) // 2
        at_b = aligned(b * CHUNK, CHUNK, CHUNK)
        oo_copy(q).wait()
        peers = pend2[b % 2, 0] + orecv2[aligned((1 - cls) * 128, 128, 128), at_b].astype(jnp.float32)
        packed[0, 0:128, at_c] = peers.astype(jnp.bfloat16)
        ii_copy(q).start()
        pend[q % RING] = pend2[b % 2, 1] + orecv2[aligned(cls * 128, 128, 128), at_b].astype(jnp.float32)

    def add_pair(q):
        flow, at_c = place(q)
        ib_copy(q).wait()
        total = ipend[q % steps] + irecv[flow, :, at_c].astype(jnp.float32)
        rows[flow, class_own, at_c] = total.astype(jnp.bfloat16)
        start(zb_copies(q))
        zb_local(q).start()

    def combine(q):
        flow, at_c = place(q)
        wait(zb_copies(q))
        zb_local(q).wait()
        block = back[flow, :, at_c]
        away = mm(comb[flow, 0, other, 0:320], block) + mm(comb[flow, 1, other, 0:320], block)
        dense[flow, 0:128, at_c] = away.astype(jnp.bfloat16)
        ob_copy(q).start()
        pend[q % RING] = mm(comb[flow, 0, own, 0:320], block) + mm(comb[flow, 1, own, 0:320], block)

    def add_outer(q):
        flow, at_c = place(q)
        slot = q % RING
        rows_mine, rows_peer = aligned(x * 64, 64, 64), aligned((1 - x) * 64, 64, 64)

        @pl.when(plain(q))
        def _():
            ob_copy(q).wait()
            pend[slot] += orecv[flow, :, at_c].astype(jnp.float32)

        @pl.when(jnp.logical_not(plain(q)))
        def _():
            ii_copy(q).wait()
            pend[slot] += irecv[1, 0:128, at_c].astype(jnp.float32)

        at_d = aligned(x * width + (q % steps) * CHUNK, CHUNK, CHUNK)

        @pl.when(flow == 0)
        def _():
            grad[:, at_d] = pend[slot, rows_mine]

        @pl.when(flow == 1)
        def _():
            pend[slot] += raw[:, at_c].astype(jnp.float32)
            fwd_out[:, at_d] = pend[slot, rows_mine].astype(jnp.bfloat16)

        dense[flow, 128:192, at_c] = pend[slot, rows_peer].astype(jnp.bfloat16)
        xb_copy(q).start()

    def finish(q):
        flow, at_c = place(q)
        at_d = aligned((1 - x) * width + (q % steps) * CHUNK, CHUNK, CHUNK)
        xb_copy(q).wait()

        @pl.when(flow == 0)
        def _():
            grad[:, at_d] = xrecv[0, :, at_c].astype(jnp.float32)

        @pl.when(flow == 1)
        def _():
            fwd_out[:, at_d] = xrecv[1, :, at_c]

    def each(first, last, stage):
        def one(q, carry):
            stage(q)
            return carry

        lax.fori_loop(first, last, one, 0)

    lax.fori_loop(0, steps, out_grad, 0)
    each(0, 4, add_pair)
    each(0, 3, combine)
    add_outer(0)

    def gated(h):
        for k in range(2):
            p_copy(1 + k, h).wait()

        def some(i, carry):
            start_row = (1 - cls if h == 0 else cls) * 320
            at_i = aligned(start_row + i * 160, 160, 160)
            gate = acc[0, 0, at_i] + precv[1, at_i].astype(jnp.float32)
            upper = acc[1, 0, at_i] + precv[2, at_i].astype(jnp.float32)
            hid[0, at_i] = (gate * jax.nn.sigmoid(gate) * upper).astype(jnp.bfloat16)
            return carry

        lax.fori_loop(0, 2, some, 0)
        hid_copy(h).start()

    gated(0)
    add_pair(4)
    combine(3)
    add_outer(1)
    gated(1)
    gres_copy.start()
    add_pair(5)
    combine(4)
    add_outer(2)
    hid_copy(0).wait()

    def step(t, carry):
        @pl.when(t < steps)
        def _():
            out_rows(t)

        def stage(q, least, do):
            @pl.when((q >= least) & (q < 2 * steps))
            def _():
                do(q)

        def two_ways(q, least, do, do_odd):
            @pl.when((q >= least) & (q < 2 * steps) & plain(q))
            def _():
                do(q)

            @pl.when((q >= steps) & (q < 2 * steps) & jnp.logical_not(plain(q)))
            def _():
                do_odd(q)

        two_ways(t + steps - LAG, 6, add_pair, combine_all)

        two_ways(t + steps - 2 * LAG, 5, combine, add_outer_all)
        stage(t + steps - 3 * LAG, 3, add_outer)
        stage(t + steps - 4 * LAG, max(0, steps - 4 * LAG), finish)

        @pl.when(t == 4 * LAG - 1)
        def _():
            wait(u_loads)
            gres_copy.wait()
            bwd_out[:, cols_peer] = gres[...]

            def norm_back(i, carry):
                at_i = aligned(i * 16, 16, 16)
                at_u = [aligned(128 + k * 64 + i * 16, 16, 16) for k in range(2)]
                u = jnp.concatenate([packed[0, at_k] for at_k in at_u], axis=1).astype(jnp.float32)
                r = lax.rsqrt(jnp.mean(u * u, axis=1, keepdims=True) + EPSILON)
                h = grad[at_i] * gains[...]
                along = jnp.mean(h * u, axis=1, keepdims=True)
                result = r * h - u * (r * r * r * along)
                bwd_out[at_i] = (bwd_out[at_i].astype(jnp.float32) + result).astype(jnp.bfloat16)
                return carry

            lax.fori_loop(0, 4, norm_back, 0)

        return carry

    lax.fori_loop(0, steps + 4 * LAG, step, 0)


def on_device(
    fwd_in, gains, gate_weight, up_weight, down_weight, fwd_routes, fwd_probs,
    bwd_grad, bwd_input, bwd_routes, bwd_probs, bwd_stash,
):
    depth = fwd_in.shape[2]
    width = depth // 2
    hidden = gate_weight.shape[2]
    r = np.arange(384)
    goal = np.where(r < 320, (r // 80) * 2 * CAP + r % CAP + 1000 * ((r % 80) // CAP), -1000000)
    goal = jnp.asarray(goal.reshape(1, 384), jnp.float32)
    bf, f32 = jnp.bfloat16, jnp.float32
    vmem, hbm = pl.BlockSpec(memory_space=pltpu.VMEM), pl.BlockSpec(memory_space=pl.ANY)
    dma = pltpu.SemaphoreType.DMA
    steps = width // CHUNK
    two = 2 * steps
    scratch = [
        pltpu.VMEM((64, 128), f32),
        pltpu.VMEM((512, 128), f32),
        pltpu.VMEM((24, 128), f32),
        pltpu.VMEM((128, 128), f32),
        pltpu.VMEM((128, width), bf),
        pltpu.VMEM((2, 256, width), bf),
        pltpu.VMEM((2, 320, width), bf),
        pltpu.VMEM((2, 640, width), bf),
        pltpu.VMEM((2, width, hidden), bf),
        pltpu.VMEM((2, width, hidden), bf),
        pltpu.VMEM((hidden, width), bf),
        pltpu.VMEM((hidden, width), bf),
        pltpu.VMEM((640, 2 * hidden), bf),
        pltpu.VMEM((2, 2, 640, hidden), f32),
        pltpu.VMEM((3, 640, hidden), bf),
        pltpu.VMEM((3, 640, hidden), bf),
        pltpu.VMEM((2, 2, 640, hidden), bf),
        pltpu.VMEM((2, 640, hidden), bf),
        pltpu.VMEM((2, 320, width), bf),
        pltpu.VMEM((steps, 320, CHUNK), f32),
        pltpu.VMEM((2, 320, width), bf),
        pltpu.VMEM((320, steps // 2 * CHUNK), bf),
        pltpu.VMEM((RING, 128, CHUNK), f32),
        pltpu.VMEM((2, 2, 128, CHUNK), f32),
        pltpu.VMEM((2, 128, width), bf),
        pltpu.VMEM((256, steps // 2 * CHUNK), bf),
        pltpu.VMEM((2, 64, width), bf),
        pltpu.VMEM((64, depth), f32),
        pltpu.VMEM((64, width), bf),
        pltpu.VMEM((2, 384, 256), bf),
        pltpu.VMEM((3, 2, 256, 384), bf),
        dma((2, PARTS, 2)), dma((2, PARTS, 2)),
        dma, dma,
        dma((2,)), dma((2,)),
        dma((7,)), dma((7,)),
        dma((2, PARTS)), dma((2, PARTS)),
        dma((2, PARTS, 3)), dma((2, PARTS, 3)),
        dma((2, PARTS)), dma((2, PARTS)),
        dma((2, width // CHUNK)), dma((2, width // CHUNK)),
        dma, dma,
        dma((3, 2)), dma((3, 2)),
        dma((2,)), dma((2,)),
        dma((2,)), dma((2,)),
        dma((two,)), dma((two,)),
        dma((steps // 2, 2, 3)), dma((steps // 2, 2, 3)), dma((steps // 2, 2)),
        dma((two, 3)), dma((two, 3)),
        dma((two,)), dma((two,)),
        dma((two,)), dma((two,)),
        dma((7,)), dma((2, PARTS)), dma((two,)),
    ]
    outs = pl.pallas_call(
        kernel,
        out_shape=jax.ShapeDtypeStruct((2, 64, depth), bf),
        in_specs=[vmem, hbm, vmem, hbm, hbm, hbm, vmem, vmem, vmem, vmem, hbm, hbm, vmem],
        out_specs=vmem,
        scratch_shapes=scratch,
        compiler_params=pltpu.CompilerParams(
            collective_id=0, has_side_effects=True, vmem_limit_bytes=63 * 1024 * 1024
        ),
        name="routed_experts",
    )(
        fwd_in[0], bwd_grad[0], gains, gate_weight[0], up_weight[0], down_weight[0],
        fwd_routes[0].T, fwd_probs[0].T, bwd_routes[0].T, bwd_probs[0].T, bwd_input[0], bwd_stash[0], goal,
    )
    return (outs[0:1], outs[1:2])


def solution(mesh):
    rows = P("section", "expert", None)
    cols = P("section", None, "expert")
    return jax.shard_map(
        on_device,
        mesh=mesh,
        in_specs=(rows, P("section", None), cols, cols, rows, rows, rows, rows, rows, rows, rows, rows),
        out_specs=(rows, rows),
        check_vma=False,
    )
```
